512 devices in a mesh: dp: 64 (over y, x, core), fsdp: 8 (over z).
Axes of the slice: x: 4, y: 8, z: 8, core: 2. Of those that a mesh axis runs over, the one named last changes fastest.
Arguments:
- queries: bfloat16 [65536, 3584], P(('dp', 'fsdp')), may hold values from -60 to 60
- keys: bfloat16 [65536, 512], P(('dp', 'fsdp')), may hold values from -6 to 6
- values: bfloat16 [65536, 512], P(('dp', 'fsdp')), may hold values from -6 to 6
- out_grad: bfloat16 [65536, 3584], P(('dp', 'fsdp')), may hold values from -6 to 6
- doc_first: int32 [512, 2], replicated, may hold values from 0 to 1, as said below
- doc_valid: int32 [512, 2], replicated, may hold values from 1 to 64
- move_plan: int32 [3, 512, 2], replicated, may hold values from 0 to 1, as said below
Outputs:
- attended: bfloat16 [65536, 3584], P(('dp', 'fsdp'))
- query_grad: bfloat16 [65536, 3584], P(('dp', 'fsdp'))
- key_grad: bfloat16 [65536, 512], P(('dp', 'fsdp'))
- value_grad: bfloat16 [65536, 512], P(('dp', 'fsdp'))
The draws below stay inside these ranges and needn't reach their ends.
Inputs may be any that keep to these rules, and one draw needn't show every extreme that they name: `doc_first`: block 0 of every micro-batch begins a document; a document covers the blocks from its first block up to the next document's first block; all its blocks but the last have 64 live rows. `move_plan`: A flag is equal for a micro-batch and its partner of the section; the flagged blocks of a micro-batch at a section never include block 0 and form a suffix that starts a document in both micro-batches as they stand at that section.
All inputs are finite; a program needn't handle non-finite values.
Results may differ from the reference program's by a relative error of at most 0.013.
Values may be sent and summed in bfloat16 or wider, within the bound.
No kernel may reach another device: no remote copies, remote signals or barrier semaphores. Data moves between devices by JAX's collectives and lax.ppermute only.
A program may use at most 64 MiB of HBM per device.

```python
import jax
import jax.numpy as jnp
from jax import lax

HD = 128
KVH = 4
GROUP = 7
QH = 28
BLOCK = 64
BLOCKS = 2
SECTIONS = 3
SEQ = 128
MICRO = 512
TOKENS = 65536
N_DP = 64
N_FSDP = 8


def section_partner_drawn(section_idx):
    near_bits = N_FSDP.bit_length() - 1
    far_bits = N_DP.bit_length() - 1
    if section_idx == 0:
        shift_bits = 0
    elif section_idx == 1:
        shift_bits = near_bits
    else:
        shift_bits = near_bits + far_bits - 1
    micro_ids = jnp.arange(MICRO, dtype=jnp.int32)
    return jnp.bitwise_xor(micro_ids, 1 << shift_bits)


def doc_layout(key):
    key_starts, key_tail, key_pick, key_coin = jax.random.split(key, 4)
    starts = jax.random.randint(key_starts, (MICRO, BLOCKS), 0, 2).astype(jnp.int32)
    starts = starts.at[:, 0].set(1)
    index = jnp.arange(BLOCKS, dtype=jnp.int32)[None, :]
    first = lax.cummax(jnp.where(starts == 1, index, 0), axis=1)
    following = jnp.concatenate([starts[:, 1:], jnp.ones((MICRO, 1), jnp.int32)], 1)
    tail = jax.random.randint(key_tail, (MICRO, BLOCKS), 1, BLOCK + 1).astype(jnp.int32)
    valid = jnp.where(following == 1, tail, BLOCK)
    valid = valid.at[0, BLOCKS - 1].set(BLOCK)
    micro_ids = jnp.arange(MICRO, dtype=jnp.int32)
    state = first
    flags = []
    for section_idx in range(SECTIONS):
        partner = section_partner_drawn(section_idx)
        lowest = jnp.minimum(micro_ids, partner)
        pick = jax.random.randint(jax.random.fold_in(key_pick, section_idx), (MICRO, BLOCKS), 0, 1024).astype(jnp.int32)[lowest]
        coin = jax.random.randint(jax.random.fold_in(key_coin, section_idx), (MICRO,), 0, 4).astype(jnp.int32)[lowest]
        other = state[partner]
        common = (state == index) & (other == index) & (index >= 1)
        score = jnp.where(common, pick * BLOCKS + index, -1)
        best = jnp.max(score, axis=1)
        cutoff = jnp.where((best >= 0) & (coin > 0), best % BLOCKS, BLOCKS)
        flag = (index >= cutoff[:, None]).astype(jnp.int32)
        state = jnp.where(flag == 1, other, state)
        flags.append(flag)
    return (first, valid, jnp.stack(flags))


def key_table(key):
    base = jax.random.fold_in(key, 29)
    return jnp.clip(jax.random.normal(base, (TOKENS, KVH * HD), jnp.float32), -6.0, 6.0)


def draw_doc_first(key, part):
    return doc_layout(key)[0]


def draw_doc_valid(key, part):
    return doc_layout(key)[1]


def draw_move_plan(key, part):
    return doc_layout(key)[2]


def draw_keys(key, part):
    return key_table(key).astype(jnp.bfloat16)


def draw_queries(key, part):
    key = jax.random.fold_in(key, 3)
    drawn = jnp.clip(jax.random.normal(key, (TOKENS, QH * HD), jnp.float32), -6.0, 6.0)
    return drawn.astype(jnp.bfloat16)


def block_scale(rng, shape, cuts, low, high):
    factor_of = 1.0
    for axis_at, shards_of in cuts:
        draws = jax.random.uniform(jax.random.fold_in(jax.random.fold_in(rng, 6), axis_at), (shards_of,), jnp.float32, low / len(cuts), high / len(cuts))
        factor_of = factor_of * jnp.repeat(jnp.exp(draws), shape[axis_at] // shards_of).reshape((-1,) + (1,) * (len(shape) - 1 - axis_at))
    return factor_of


def bell_draw(key, dims, spread, bound, cuts=(), held_as=jnp.bfloat16):
    values = jax.random.normal(key, dims, jnp.float32) * spread
    if len(cuts) > 0:
        values = block_scale(key, dims, cuts, -0.22, 0.18) * values
    return jnp.clip(values, min=-bound, max=bound).astype(held_as)


def setup_inputs(seed: int = 0) -> dict:
    key_list = jax.random.split(jax.random.key(seed), 8)
    queries = draw_queries(jax.random.fold_in(key_list[7], 71), 0)
    keys = draw_keys(jax.random.fold_in(key_list[7], 71), 0)
    values = bell_draw(key_list[2], (TOKENS, KVH * HD), 1.0, 6.0, ((0, 512),))
    out_grad = bell_draw(key_list[3], (TOKENS, QH * HD), 1.0, 6.0, ((0, 512),))
    doc_first = draw_doc_first(jax.random.fold_in(key_list[7], 71), 0)
    doc_valid = draw_doc_valid(jax.random.fold_in(key_list[7], 71), 0)
    move_plan = draw_move_plan(jax.random.fold_in(key_list[7], 71), 0)
    return dict(queries=queries, keys=keys, values=values, out_grad=out_grad, doc_first=doc_first, doc_valid=doc_valid, move_plan=move_plan)


def section_partner(section_idx):
    near_bits = N_FSDP.bit_length() - 1
    far_bits = N_DP.bit_length() - 1
    if section_idx == 0:
        shift_bits = 0
    elif section_idx == 1:
        shift_bits = near_bits
    else:
        shift_bits = near_bits + far_bits - 1
    micro_ids = jnp.arange(MICRO, dtype=jnp.int32)
    return jnp.bitwise_xor(micro_ids, 1 << shift_bits)


def attend_all(qm, km, vm, dm, allow):
    scale = 1.0 / (HD ** 0.5)
    count = qm.shape[0]
    outs, dqs, dks, dvs = [], [], [], []
    for head_idx in range(KVH):
        lower = head_idx * GROUP * HD
        qh = qm[:, lower:lower + GROUP * HD].reshape(count, GROUP, HD).astype(jnp.float32)
        dh = dm[:, lower:lower + GROUP * HD].reshape(count, GROUP, HD).astype(jnp.float32)
        kh = km[:, head_idx * HD:(head_idx + 1) * HD].astype(jnp.float32)
        vh = vm[:, head_idx * HD:(head_idx + 1) * HD].astype(jnp.float32)
        score = jnp.einsum('rgd,sd->grs', qh, kh) * scale
        masked = jnp.where(allow[None], score, -1e30)
        top = jnp.max(masked, axis=-1, keepdims=True)
        weights = jnp.exp(masked - top)
        probs = weights / jnp.sum(weights, axis=-1, keepdims=True)
        probs_b = probs.astype(jnp.bfloat16).astype(jnp.float32)
        outs.append(jnp.einsum('grs,sd->rgd', probs_b, vh).astype(jnp.bfloat16).reshape(count, GROUP * HD))
        dprob = jnp.einsum('rgd,sd->grs', dh, vh)
        delta = jnp.sum(probs * dprob, axis=-1, keepdims=True)
        dscore = (probs * (dprob - delta) * scale).astype(jnp.bfloat16).astype(jnp.float32)
        dqs.append(jnp.einsum('grs,sd->rgd', dscore, kh).astype(jnp.bfloat16).reshape(count, GROUP * HD))
        dks.append(jnp.einsum('grs,rgd->sd', dscore, qh))
        dvs.append(jnp.einsum('grs,rgd->sd', probs_b, dh))
    return (jnp.concatenate(outs, 1), jnp.concatenate(dqs, 1),
            jnp.concatenate(dks, 1), jnp.concatenate(dvs, 1))


def reference(queries, keys, values, out_grad, doc_first, doc_valid, move_plan):
    micro_ids = jnp.arange(MICRO, dtype=jnp.int32)
    source = jnp.broadcast_to(micro_ids[:, None], (MICRO, BLOCKS)).astype(jnp.int32)
    for section_idx in range(SECTIONS):
        partner = section_partner(section_idx)
        source = jnp.where(move_plan[section_idx] == 1, source[partner], source)
    block_ids = jnp.broadcast_to(jnp.arange(BLOCKS, dtype=jnp.int32)[None, :], (MICRO, BLOCKS))

    def moved(array):
        view = array.reshape(MICRO, BLOCKS, BLOCK, array.shape[-1])
        return view[source, block_ids].reshape(MICRO, SEQ, array.shape[-1])

    first = doc_first[source, block_ids]
    valid = doc_valid[source, block_ids]
    positions = jnp.arange(SEQ, dtype=jnp.int32)

    def one_batch(operands):
        qm, km, vm, dm, first_row, valid_row = operands
        start = jnp.repeat(first_row, BLOCK) * BLOCK
        live = (positions % BLOCK) < jnp.repeat(valid_row, BLOCK)
        allow = (positions[None, :] >= start[:, None]) & (positions[None, :] <= positions[:, None]) & live[None, :]
        out, dq, dk, dv = attend_all(qm, km, vm, dm, allow)
        return out, dq, dk.astype(jnp.bfloat16), dv.astype(jnp.bfloat16)

    out, dq, dk, dv = lax.map(one_batch, (moved(queries), moved(keys), moved(values), moved(out_grad), first, valid))
    return (out.reshape(TOKENS, QH * HD), dq.reshape(TOKENS, QH * HD),
            dk.reshape(TOKENS, KVH * HD), dv.reshape(TOKENS, KVH * HD))
```

```python
import functools

import jax
import jax.numpy as jnp
from jax import lax
from jax.experimental import pallas as pl
from jax.experimental.pallas import tpu as pltpu
from jax.sharding import PartitionSpec as P

HD = 128
KVH = 4
GROUP = 7
BLOCK = 64
SEQ = 2 * BLOCK
SCALE = 1.0 / HD**0.5
PAIR = 2 * GROUP * HD
TRI = GROUP * BLOCK
DIAG = 16
SIDE = 2 * BLOCK
ROWS = TRI + DIAG + 4 * SIDE
AT = TRI + DIAG
VMEM_LIMIT = 48 * 1024 * 1024

NT = (((1,), (1,)), ((), ()))
NN = (((1,), (0,)), ((), ()))
TN = (((0,), (0,)), ((), ()))


def mm(a, b, dims):
    return lax.dot_general(a, b, dims, preferred_element_type=jnp.float32)


def iota(shape, dim):
    return lax.broadcasted_iota(jnp.int32, shape, dim)


def fold_matrix():
    shape = (BLOCK, 2 * BLOCK)
    return jnp.where((iota(shape, 1) & (BLOCK - 1)) == iota(shape, 0), 1.0, 0.0).astype(jnp.bfloat16)


def turn(fold, pair):
    low = iota(pair.shape, 1) < BLOCK
    zero = jnp.zeros_like(pair)
    split = jnp.concatenate([jnp.where(low, pair, zero), jnp.where(low, zero, pair)], 0)
    return mm(fold, split, NT)


def pack_kernel(chunk, head_rows, valid_ref, q_ref, k_ref, v_ref, g_ref, *refs):
    other_ref = refs[0] if head_rows else None
    pack_ref, qbd, gbd = refs[-3:]
    zero = jnp.zeros((BLOCK, HD), jnp.bfloat16)
    for full, ref in ((qbd, q_ref), (gbd, g_ref)):
        for h in range(GROUP):
            r = h * 2 * BLOCK
            full[r : r + BLOCK, 0:HD] = ref[:, h * HD : (h + 1) * HD]
            full[r : r + BLOCK, HD:] = zero
            full[r + BLOCK : r + 2 * BLOCK, 0:HD] = zero
            full[r + BLOCK : r + 2 * BLOCK, HD:] = ref[:, (GROUP + h) * HD : (GROUP + h + 1) * HD]
    wide = (BLOCK, GROUP * 2 * BLOCK)
    key_pos = iota(wide, 0)
    query_pos = iota(wide, 1) & (BLOCK - 1)
    allow = (key_pos <= query_pos) & (key_pos < valid_ref[0])
    score = jnp.where(allow, mm(k_ref[...], qbd[...], NT) * SCALE, -1e30)
    weights = jnp.exp(score - jnp.max(score, axis=0, keepdims=True))
    probs = weights / jnp.sum(weights, axis=0, keepdims=True)
    probs_b = probs.astype(jnp.bfloat16)
    dprob = mm(v_ref[...], gbd[...], NT)
    delta = jnp.sum(probs * dprob, axis=0, keepdims=True)
    dscore = (probs * (dprob - delta) * SCALE).astype(jnp.bfloat16)
    dv = mm(probs_b, gbd[...], NN).astype(jnp.bfloat16)
    dk = mm(dscore, qbd[...], NN).astype(jnp.bfloat16)

    fold = fold_matrix()
    square = (BLOCK, 2 * BLOCK)
    row, lane = iota(square, 0), iota(square, 1) & (BLOCK - 1)
    diag = []
    for h in range(GROUP):
        cut = slice(h * 2 * BLOCK, (h + 1) * 2 * BLOCK)
        ds = dscore[:, cut]
        pack_ref[h * BLOCK : (h + 1) * BLOCK, :] = jnp.where(
            row <= lane, probs_b[:, cut].astype(jnp.float32), turn(fold, ds)
        ).astype(jnp.bfloat16)
        diag.append(
            jnp.sum(jnp.where(row == lane, ds.astype(jnp.float32), 0.0), axis=0, keepdims=True)
        )
    diag.append(jnp.zeros((DIAG - GROUP, 2 * BLOCK), jnp.float32))
    pack_ref[TRI:AT, :] = jnp.concatenate(diag, 0).astype(jnp.bfloat16)
    for i, part in enumerate((k_ref[...], v_ref[...], dk, dv)):
        for j in range(2):
            r = AT + i * SIDE + j * BLOCK
            pack_ref[r : r + BLOCK, :] = part[:, j * HD : (j + 1) * HD]
    if head_rows:
        pack_ref[ROWS:, :] = other_ref[...]


def make_pack(chunk, valid, q, k, v, g, other=None):
    rows = ROWS if other is None else 2 * ROWS
    wide = pl.BlockSpec((BLOCK, PAIR), lambda i: (1, chunk))
    thin = pl.BlockSpec((BLOCK, 2 * HD), lambda i: (1, chunk))
    specs = [pl.BlockSpec(memory_space=pltpu.SMEM), wide, thin, thin, wide]
    args = [valid, q, k, v, g]
    if other is not None:
        specs.append(pl.BlockSpec((ROWS, HD), lambda i: (0, 0)))
        args.append(other)
    return pl.pallas_call(
        functools.partial(pack_kernel, chunk, other is not None),
        grid=(1,),
        out_shape=jax.ShapeDtypeStruct((rows, HD), jnp.bfloat16),
        in_specs=specs,
        out_specs=pl.BlockSpec((rows, HD), lambda i: (0, 0)),
        scratch_shapes=[pltpu.VMEM((GROUP * 2 * BLOCK, 2 * HD), jnp.bfloat16)] * 2,
        compiler_params=pltpu.CompilerParams(vmem_limit_bytes=VMEM_LIMIT),
        cost_estimate=pl.CostEstimate(
            flops=8 * BLOCK * GROUP * 2 * BLOCK * 2 * HD, bytes_accessed=1 << 20, transcendentals=0
        ),
        name="pack_rows",
    )(*args)


def own_kernel(first_ref, valid_ref, q_ref, k_ref, v_ref, g_ref, o_ref, dq_ref, dk_ref, dv_ref):
    k, v = k_ref[...], v_ref[...]
    q = jnp.concatenate([q_ref[:, h * HD : (h + 1) * HD] for h in range(GROUP)], 0)
    g = jnp.concatenate([g_ref[:, h * HD : (h + 1) * HD] for h in range(GROUP)], 0)
    wide = (SEQ, GROUP * SEQ)
    key_pos = iota(wide, 0)
    query_pos = iota(wide, 1) & (SEQ - 1)
    start = jnp.where(query_pos < BLOCK, first_ref[0], first_ref[1]) * BLOCK
    live = jnp.where(key_pos < BLOCK, valid_ref[0], valid_ref[1])
    allow = (key_pos >= start) & (key_pos <= query_pos) & ((key_pos & (BLOCK - 1)) < live)
    score = jnp.where(allow, mm(k, q, NT) * SCALE, -1e30)
    weights = jnp.exp(score - jnp.max(score, axis=0, keepdims=True))
    probs = weights / jnp.sum(weights, axis=0, keepdims=True)
    probs_b = probs.astype(jnp.bfloat16)
    dprob = mm(v, g, NT)
    delta = jnp.sum(probs * dprob, axis=0, keepdims=True)
    dscore = (probs * (dprob - delta) * SCALE).astype(jnp.bfloat16)
    dv_ref[...] = mm(probs_b, g, NN).astype(jnp.bfloat16)
    dk_ref[...] = mm(dscore, q, NN).astype(jnp.bfloat16)
    for h in range(GROUP):
        cut = slice(h * SEQ, (h + 1) * SEQ)
        o_ref[:, h * HD : (h + 1) * HD] = mm(probs_b[:, cut], v, TN).astype(jnp.bfloat16)
        dq_ref[:, h * HD : (h + 1) * HD] = mm(dscore[:, cut], k, TN).astype(jnp.bfloat16)


def own_attention(first, valid, q, k, v, g):
    wide = pl.BlockSpec((SEQ, GROUP * HD), lambda i: (0, i))
    thin = pl.BlockSpec((SEQ, HD), lambda i: (0, i))
    smem = pl.BlockSpec(memory_space=pltpu.SMEM)
    return pl.pallas_call(
        own_kernel,
        grid=(KVH,),
        out_shape=[jax.ShapeDtypeStruct(x.shape, jnp.bfloat16) for x in (q, q, k, v)],
        in_specs=[smem, smem, wide, thin, thin, wide],
        out_specs=[wide, wide, thin, thin],
        compiler_params=pltpu.CompilerParams(vmem_limit_bytes=VMEM_LIMIT),
        cost_estimate=pl.CostEstimate(
            flops=12 * KVH * GROUP * SEQ * SEQ * HD, bytes_accessed=4 << 20, transcendentals=0
        ),
        name="own_attention",
    )(first, valid, q, k, v, g)


def place_kernel(chunk, sources, pick_ref, *refs):
    packs = refs[:sources]
    o_ref, dq_ref, dk_ref, dv_ref, pack, o_buf, dq_buf, side, sem = refs[sources + 4 :]
    pick = pick_ref[0]
    for i, ref in enumerate(packs):

        @pl.when(pick == i)
        def _():
            got = pltpu.make_async_copy(ref, pack, sem.at[4])
            got.start()
            got.wait()

    @pl.when(pick < sources)
    def _():
        fold = fold_matrix()
        square = (BLOCK, 2 * BLOCK)
        row, lane = iota(square, 0), iota(square, 1) & (BLOCK - 1)
        zero = jnp.zeros((BLOCK, HD), jnp.bfloat16)

        def spread(i):
            r = AT + i * SIDE
            return jnp.concatenate(
                [
                    jnp.concatenate([pack[r : r + BLOCK, :], zero], 1),
                    jnp.concatenate([zero, pack[r + BLOCK : r + SIDE, :]], 1),
                ],
                0,
            )

        kbd, vbd = spread(0), spread(1)
        for j in range(2):
            for i in range(2):
                r = AT + (2 + i) * SIDE + j * BLOCK
                side[i, :, j * HD : (j + 1) * HD] = pack[r : r + BLOCK, :]
        diag = pack[TRI:AT, :].astype(jnp.float32)
        probs, dscore = [], []
        for h in range(GROUP):
            both = pack[h * BLOCK : (h + 1) * BLOCK, :].astype(jnp.float32)
            upper = jnp.where(row <= lane, both, 0.0).astype(jnp.bfloat16)
            probs.append(turn(fold, upper).astype(jnp.bfloat16))
            line = jnp.where(row == lane, diag[h : h + 1, :], 0.0)
            dscore.append(jnp.where(row > lane, both, line).astype(jnp.bfloat16))
        out = mm(jnp.concatenate(probs, 0), vbd, NN).astype(jnp.bfloat16)
        dq = mm(jnp.concatenate(dscore, 0), kbd, NN).astype(jnp.bfloat16)
        for buf, val in ((o_buf, out), (dq_buf, dq)):
            for h in range(GROUP):
                for j in range(2):
                    at = (j * GROUP + h) * HD
                    buf[:, at : at + HD] = val[h * BLOCK : (h + 1) * BLOCK, j * HD : (j + 1) * HD]
        rows = pl.ds(BLOCK, BLOCK)
        copies = [
            pltpu.make_async_copy(o_buf, o_ref.at[rows, pl.ds(chunk * PAIR, PAIR)], sem.at[0]),
            pltpu.make_async_copy(dq_buf, dq_ref.at[rows, pl.ds(chunk * PAIR, PAIR)], sem.at[1]),
            pltpu.make_async_copy(
                side.at[0], dk_ref.at[rows, pl.ds(chunk * 2 * HD, 2 * HD)], sem.at[2]
            ),
            pltpu.make_async_copy(
                side.at[1], dv_ref.at[rows, pl.ds(chunk * 2 * HD, 2 * HD)], sem.at[3]
            ),
        ]
        for c in copies:
            c.start()
        for c in copies:
            c.wait()


def place(chunk, pick, packs, outs):
    n = len(packs)
    return pl.pallas_call(
        functools.partial(place_kernel, chunk, n),
        out_shape=[jax.ShapeDtypeStruct(x.shape, x.dtype) for x in outs],
        in_specs=[pl.BlockSpec(memory_space=pltpu.SMEM)] + [pl.BlockSpec(memory_space=pl.ANY)] * (n + 4),
        out_specs=[pl.BlockSpec(memory_space=pl.ANY)] * 4,
        scratch_shapes=[
            pltpu.VMEM((ROWS, HD), jnp.bfloat16),
            pltpu.VMEM((BLOCK, PAIR), jnp.bfloat16),
            pltpu.VMEM((BLOCK, PAIR), jnp.bfloat16),
            pltpu.VMEM((2, BLOCK, 2 * HD), jnp.bfloat16),
            pltpu.SemaphoreType.DMA((5,)),
        ],
        input_output_aliases={1 + n + i: i for i in range(4)},
        compiler_params=pltpu.CompilerParams(vmem_limit_bytes=VMEM_LIMIT),
        cost_estimate=pl.CostEstimate(
            flops=8 * GROUP * BLOCK * 2 * BLOCK * 2 * HD, bytes_accessed=1 << 20, transcendentals=0
        ),
        name="place_rows",
    )(pick, *packs, *outs)


def swap(shard, axis, bit):
    return lax.ppermute(shard, axis, [(i, i ^ 1 << bit) for i in range(lax.axis_size(axis))])


def body(queries, keys, values, out_grad, doc_first, doc_valid, move_plan):
    near = lax.axis_size("fsdp")
    top = lax.axis_size("dp").bit_length() - 2
    micro = lax.axis_index("dp") * near + lax.axis_index("fsdp")
    across = jnp.bitwise_xor(micro, near << top)
    first, valid = doc_first[micro], doc_valid[micro]
    mine, theirs = move_plan[:, micro, 1], move_plan[:, across, 1]
    f0, f1, f2 = mine[0] == 1, mine[1] == 1, mine[2] == 1
    g0, g1 = theirs[0] == 1, theirs[1] == 1

    args = (queries, keys, values, out_grad)
    pack_b = make_pack(1, valid[1:], *args)
    far_b = swap(pack_b, "dp", top)
    pack = make_pack(0, valid[1:], *args, other=pack_b)
    outs = own_attention(first, valid, *args)
    pack = jnp.where(f0, swap(pack, "fsdp", 0), pack)
    pack = jnp.where(f1, swap(pack, "dp", 0), pack)
    pack_a, pack_b = pack[:ROWS], pack[ROWS:]
    far_a = swap(pack_a, "dp", top)
    far_b = jnp.where(g0, swap(far_b, "fsdp", 0), far_b)
    near_b = swap(far_b, "dp", 0)
    still = ~(f0 | f1 | f2)
    pick_b = jnp.where(still, 3, jnp.where(f2, jnp.where(g1, 2, 1), 0)).astype(jnp.int32)
    outs = place(1, pick_b[None], (pack_b, far_b, near_b), outs)
    pick_a = jnp.where(still, 2, jnp.where(f2, 1, 0)).astype(jnp.int32)
    return tuple(place(0, pick_a[None], (pack_a, far_a), outs))


def solution(mesh):
    rows = P(("dp", "fsdp"), None)
    return jax.shard_map(
        body,
        mesh=mesh,
        in_specs=(rows,) * 4 + (P(),) * 3,
        out_specs=(rows,) * 4,
        check_vma=False,
    )
```

```python
import functools

import jax
import jax.numpy as jnp
from jax import lax
from jax.experimental import pallas as pl
from jax.experimental.pallas import tpu as pltpu
from jax.sharding import PartitionSpec as P

HD = 128
KVH = 4
GROUP = 7
BLOCK = 64
SEQ = 2 * BLOCK
SCALE = 1.0 / HD**0.5
PAIR = 2 * GROUP * HD
TRI = GROUP * BLOCK
DIAG = 16
SIDE = 2 * BLOCK
ROWS = TRI + DIAG + 4 * SIDE
AT = TRI + DIAG
VMEM_LIMIT = 40 * 1024 * 1024
PACK_LIMIT = 48 * 1024 * 1024

NT = (((1,), (1,)), ((), ()))
NN = (((1,), (0,)), ((), ()))
TN = (((0,), (0,)), ((), ()))


def mm(a, b, dims):
    return lax.dot_general(a, b, dims, preferred_element_type=jnp.float32)


def iota(shape, dim):
    return lax.broadcasted_iota(jnp.int32, shape, dim)


def fold_matrix():
    shape = (BLOCK, 2 * BLOCK)
    return jnp.where((iota(shape, 1) & (BLOCK - 1)) == iota(shape, 0), 1.0, 0.0).astype(jnp.bfloat16)


def turn(fold, pair):
    low = iota(pair.shape, 1) < BLOCK
    zero = jnp.zeros_like(pair)
    split = jnp.concatenate([jnp.where(low, pair, zero), jnp.where(low, zero, pair)], 0)
    return mm(fold, split, NT)


def read_moves(plan_ref, near, core, far):
    me = lax.axis_index("dp") * core + lax.axis_index("fsdp")
    base = me & ~(near + far)
    z, c = [], []
    for q in range(4):
        at = base + (q & 1) * near + (q >> 1) * far
        c.append(plan_ref[1, 1, at])
        z.append(plan_ref[0, 1, at ^ (c[q] * core)])
    y = [plan_ref[2, 1, base], plan_ref[2, 1, base + near]]
    here = ((me // near) & 1) + 2 * ((me // far) & 1)

    def pick(values, index):
        out = values[0]
        for i in range(1, len(values)):
            out = jnp.where(index == i, values[i], out)
        return out

    def origin(chip):
        crossed = pick(y, chip & 1)
        passed = chip ^ (2 * crossed)
        return pick(z, passed) ^ (2 * crossed), pick(c, passed)

    branch = y[0] + 2 * y[1] + 4 * z[0] + 8 * z[1] + 16 * z[2] + 32 * z[3]
    send = [origin(here ^ step)[1] for step in range(1, 4)]
    mine, other = origin(here)
    take = jnp.where(mine == 0, other, mine + 1)
    return branch, send, take


def fill_zeros(full):
    zero = jnp.zeros((BLOCK, HD), jnp.bfloat16)
    for h in range(GROUP):
        r = h * 2 * BLOCK
        full[r : r + BLOCK, HD:] = zero
        full[r + BLOCK : r + 2 * BLOCK, 0:HD] = zero


def fill_pair(full, rows):
    for h in range(GROUP):
        r = h * 2 * BLOCK
        full[r : r + BLOCK, 0:HD] = rows[:, h * HD : (h + 1) * HD]
        full[r + BLOCK : r + 2 * BLOCK, HD:] = rows[:, (GROUP + h) * HD : (GROUP + h + 1) * HD]


def attend(q, k, v, g, allow):
    score = jnp.where(allow, mm(k, q, NT) * SCALE, -1e30)
    weights = jnp.exp(score - jnp.max(score, axis=0, keepdims=True))
    probs = weights / jnp.sum(weights, axis=0, keepdims=True)
    probs_b = probs.astype(jnp.bfloat16)
    dprob = mm(v, g, NT)
    delta = jnp.sum(probs * dprob, axis=0, keepdims=True)
    dscore = (probs * (dprob - delta) * SCALE).astype(jnp.bfloat16)
    dv = mm(probs_b, g, NN).astype(jnp.bfloat16)
    dk = mm(dscore, q, NN).astype(jnp.bfloat16)
    return probs_b, dscore, dk, dv


def block_mask(live):
    wide = (BLOCK, GROUP * 2 * BLOCK)
    key_pos = iota(wide, 0)
    query_pos = iota(wide, 1) & (BLOCK - 1)
    return (key_pos <= query_pos) & (key_pos < live)


def pack_kernel(bits, first_hbm, valid_hbm, plan_hbm, q_hbm, k_hbm, v_hbm, g_hbm, *refs):
    pack_ref, branch_ref, send_ref, facts_ref = refs[:4]
    bufs = refs[4:8]
    first_ref, valid_ref, plan_ref, qbd, gbd, sem = refs[8:]
    q_buf, k_buf, v_buf, g_buf = bufs
    words = [
        pltpu.make_async_copy(hbm, ref, sem.at[4, i])
        for i, (hbm, ref) in enumerate(
            ((plan_hbm, plan_ref), (valid_hbm, valid_ref), (first_hbm, first_ref))
        )
    ]
    copies = []
    for block, chunk in ((1, 0), (1, 1), (0, 0), (0, 1)):
        rows = pl.ds(block * BLOCK, BLOCK)
        for i, (hbm, buf) in enumerate(zip((q_hbm, k_hbm, v_hbm, g_hbm), bufs)):
            width = buf.shape[1] // 2
            at = (rows, pl.ds(chunk * width, width))
            copies.append(pltpu.make_async_copy(hbm.at[at], buf.at[at], sem.at[len(copies) // 4, i]))
    for c in words + copies:
        c.start()
    fill_zeros(qbd)
    fill_zeros(gbd)
    for c in words:
        c.wait()
    branch, send, take = read_moves(plan_ref, *bits)
    me = lax.axis_index("dp") * bits[1] + lax.axis_index("fsdp")
    branch_ref[0] = branch
    for i in range(3):
        send_ref[i] = jnp.full((1, HD), send[i], jnp.int32)
    facts = (take, jnp.where(first_ref[1, me] == 0, 1, 0), valid_ref[0, me], valid_ref[1, me])
    for i, fact in enumerate(facts):
        facts_ref[i] = jnp.full((1, HD), fact, jnp.int32)
    allow = block_mask(valid_ref[1, me])
    fold = fold_matrix()
    square = (BLOCK, 2 * BLOCK)
    row, lane = iota(square, 0), iota(square, 1) & (BLOCK - 1)
    for chunk in range(2):
        for c in copies[4 * chunk : 4 * chunk + 4]:
            c.wait()
        base = chunk * ROWS
        heads = slice(chunk * PAIR, (chunk + 1) * PAIR)
        pair = slice(chunk * 2 * HD, (chunk + 1) * 2 * HD)
        fill_pair(qbd, q_buf.at[BLOCK:, heads])
        fill_pair(gbd, g_buf.at[BLOCK:, heads])
        k, v = k_buf[BLOCK:, pair], v_buf[BLOCK:, pair]
        probs_b, dscore, dk, dv = attend(qbd[...], k, v, gbd[...], allow)
        diag = []
        for h in range(GROUP):
            cut = slice(h * 2 * BLOCK, (h + 1) * 2 * BLOCK)
            ds = dscore[:, cut]
            pack_ref[base + h * BLOCK : base + (h + 1) * BLOCK, :] = jnp.where(
                row <= lane, probs_b[:, cut].astype(jnp.float32), turn(fold, ds)
            ).astype(jnp.bfloat16)
            diag.append(
                jnp.sum(jnp.where(row == lane, ds.astype(jnp.float32), 0.0), axis=0, keepdims=True)
            )
        diag.append(jnp.zeros((DIAG - GROUP, 2 * BLOCK), jnp.float32))
        pack_ref[base + TRI : base + AT, :] = jnp.concatenate(diag, 0).astype(jnp.bfloat16)
        for i, part in enumerate((k, v, dk, dv)):
            for j in range(2):
                r = base + AT + i * SIDE + j * BLOCK
                pack_ref[r : r + BLOCK, :] = part[:, j * HD : (j + 1) * HD]
    for c in copies[8:]:
        c.wait()


def make_pack(bits, first, valid, plan, q, k, v, g):
    hbm = pl.BlockSpec(memory_space=pltpu.HBM)
    vmem = pl.BlockSpec(memory_space=pltpu.VMEM)
    return pl.pallas_call(
        functools.partial(pack_kernel, bits),
        out_shape=[
            pltpu.VMEM((2 * ROWS, HD), jnp.bfloat16),
            jax.ShapeDtypeStruct((1,), jnp.int32),
            jax.ShapeDtypeStruct((3, 1, HD), jnp.int32),
            jax.ShapeDtypeStruct((4, 1, HD), jnp.int32),
        ]
        + [pltpu.VMEM(x.shape, x.dtype) for x in (q, k, v, g)],
        in_specs=[hbm] * 7,
        out_specs=[vmem, pl.BlockSpec(memory_space=pltpu.SMEM)] + [vmem] * 6,
        scratch_shapes=[
            pltpu.SMEM(first.shape, jnp.int32),
            pltpu.SMEM(valid.shape, jnp.int32),
            pltpu.SMEM(plan.shape, jnp.int32),
            pltpu.VMEM((GROUP * 2 * BLOCK, 2 * HD), jnp.bfloat16),
            pltpu.VMEM((GROUP * 2 * BLOCK, 2 * HD), jnp.bfloat16),
            pltpu.SemaphoreType.DMA((5, 4)),
        ],
        compiler_params=pltpu.CompilerParams(vmem_limit_bytes=PACK_LIMIT),
        cost_estimate=pl.CostEstimate(
            flops=16 * BLOCK * GROUP * 2 * BLOCK * 2 * HD, bytes_accessed=3 << 20, transcendentals=0
        ),
        name="pack_rows",
    )(*(pltpu.with_memory_space_constraint(x, pltpu.HBM) for x in (first, valid, plan, q, k, v, g)))


def own_kernel(facts_ref, q_buf, k_buf, v_buf, g_buf, *refs):
    outs, news, (qbd, gbd, sem) = refs[:4], refs[4:8], refs[8:]
    o_buf, dq_buf, dk_buf, dv_buf = news

    def write(block, part, parts):
        copies = []
        for i, (buf, out) in enumerate(zip(news, outs)):
            width = buf.shape[1] // parts
            at = (pl.ds(block * BLOCK, BLOCK), pl.ds(part * width, width))
            copies.append(pltpu.make_async_copy(buf.at[at], out.at[at], sem.at[2 * block + part, i]))
            copies[-1].start()
        return copies

    joined = jnp.max(facts_ref[1]) == 1
    live = jnp.max(facts_ref[2])

    @pl.when(jnp.logical_not(joined))
    def _():
        fill_zeros(qbd)
        fill_zeros(gbd)
        allow = block_mask(live)
        copies = []
        for chunk in range(2):
            heads = slice(chunk * PAIR, (chunk + 1) * PAIR)
            pair = slice(chunk * 2 * HD, (chunk + 1) * 2 * HD)
            fill_pair(qbd, q_buf.at[0:BLOCK, heads])
            fill_pair(gbd, g_buf.at[0:BLOCK, heads])
            k, v = k_buf[0:BLOCK, pair], v_buf[0:BLOCK, pair]
            probs_b, dscore, dk, dv = attend(qbd[...], k, v, gbd[...], allow)
            dk_buf[0:BLOCK, pair] = dk
            dv_buf[0:BLOCK, pair] = dv
            for buf, squares, other in ((o_buf, probs_b, v), (dq_buf, dscore, k)):
                val = mm(squares, other, TN).astype(jnp.bfloat16)
                for h in range(GROUP):
                    for j in range(2):
                        r, at = (2 * h + j) * BLOCK, chunk * PAIR + (j * GROUP + h) * HD
                        buf[0:BLOCK, at : at + HD] = val[r : r + BLOCK, j * HD : (j + 1) * HD]
            copies += write(0, chunk, 2)
        for c in copies:
            c.wait()

    @pl.when(joined)
    def _():
        wide = (SEQ, GROUP * SEQ)
        key_pos = iota(wide, 0)
        query_pos = iota(wide, 1) & (SEQ - 1)
        live_of = jnp.where(key_pos < BLOCK, live, jnp.max(facts_ref[3]))
        allow = (key_pos <= query_pos) & ((key_pos & (BLOCK - 1)) < live_of)

        @pl.loop(0, KVH)
        def _(i):
            one = pl.ds(pl.multiple_of(i * HD, HD), HD)

            def head(h):
                return pl.ds(pl.multiple_of((i * GROUP + h) * HD, HD), HD)

            k, v = k_buf[:, one], v_buf[:, one]
            q = jnp.concatenate([q_buf[:, head(h)] for h in range(GROUP)], 0)
            g = jnp.concatenate([g_buf[:, head(h)] for h in range(GROUP)], 0)
            probs_b, dscore, dk, dv = attend(q, k, v, g, allow)
            dk_buf[:, one] = dk
            dv_buf[:, one] = dv
            for h in range(GROUP):
                cut = slice(h * SEQ, (h + 1) * SEQ)
                o_buf[:, head(h)] = mm(probs_b[:, cut], v, TN).astype(jnp.bfloat16)
                dq_buf[:, head(h)] = mm(dscore[:, cut], k, TN).astype(jnp.bfloat16)

        for c in write(0, 0, 1) + write(1, 0, 1):
            c.wait()


def own_attention(facts, q, k, v, g):
    vmem = pl.BlockSpec(memory_space=pltpu.VMEM)
    return pl.pallas_call(
        own_kernel,
        out_shape=[jax.ShapeDtypeStruct(x.shape, jnp.bfloat16) for x in (q, q, k, v)],
        in_specs=[vmem] * 5,
        out_specs=[pl.BlockSpec(memory_space=pltpu.HBM)] * 4,
        scratch_shapes=[pltpu.VMEM(x.shape, jnp.bfloat16) for x in (q, q, k, v)]
        + [pltpu.VMEM((GROUP * 2 * BLOCK, 2 * HD), jnp.bfloat16)] * 2
        + [pltpu.SemaphoreType.DMA((4, 4))],
        compiler_params=pltpu.CompilerParams(vmem_limit_bytes=VMEM_LIMIT),
        cost_estimate=pl.CostEstimate(
            flops=12 * KVH * GROUP * SEQ * SEQ * HD, bytes_accessed=4 << 20, transcendentals=0
        ),
        name="own_attention",
    )(facts, q, k, v, g)


def place_kernel(facts_ref, pack, _o, _dq, _dk, _dv, o_ref, dq_ref, dk_ref, dv_ref, o_buf, dq_buf, side, sem):
    @pl.when(jnp.max(facts_ref[1]) == 0)
    def _():
        fold = fold_matrix()
        square = (BLOCK, 2 * BLOCK)
        row, lane = iota(square, 0), iota(square, 1) & (BLOCK - 1)
        zero = jnp.zeros((BLOCK, HD), jnp.bfloat16)
        rows = pl.ds(BLOCK, BLOCK)
        copies = []
        for chunk in range(2):
            base = chunk * ROWS

            def spread(i):
                r = base + AT + i * SIDE
                return jnp.concatenate(
                    [
                        jnp.concatenate([pack[r : r + BLOCK, :], zero], 1),
                        jnp.concatenate([zero, pack[r + BLOCK : r + SIDE, :]], 1),
                    ],
                    0,
                )

            kbd, vbd = spread(0), spread(1)
            for j in range(2):
                for i in range(2):
                    r = base + AT + (2 + i) * SIDE + j * BLOCK
                    side[chunk, i, :, j * HD : (j + 1) * HD] = pack[r : r + BLOCK, :]
            diag = pack[base + TRI : base + AT, :].astype(jnp.float32)
            probs, dscore = [], []
            for h in range(GROUP):
                both = pack[base + h * BLOCK : base + (h + 1) * BLOCK, :].astype(jnp.float32)
                upper = jnp.where(row <= lane, both, 0.0).astype(jnp.bfloat16)
                probs.append(turn(fold, upper).astype(jnp.bfloat16))
                line = jnp.where(row == lane, diag[h : h + 1, :], 0.0)
                dscore.append(jnp.where(row > lane, both, line).astype(jnp.bfloat16))
            out = mm(jnp.concatenate(probs, 0), vbd, NN).astype(jnp.bfloat16)
            dq = mm(jnp.concatenate(dscore, 0), kbd, NN).astype(jnp.bfloat16)
            for buf, val in ((o_buf, out), (dq_buf, dq)):
                for h in range(GROUP):
                    for j in range(2):
                        at = (j * GROUP + h) * HD
                        buf[chunk, :, at : at + HD] = val[
                            h * BLOCK : (h + 1) * BLOCK, j * HD : (j + 1) * HD
                        ]
            heads, pair = pl.ds(chunk * PAIR, PAIR), pl.ds(chunk * 2 * HD, 2 * HD)
            for i, (buf, to) in enumerate(
                (
                    (o_buf.at[chunk], o_ref.at[rows, heads]),
                    (dq_buf.at[chunk], dq_ref.at[rows, heads]),
                    (side.at[chunk, 0], dk_ref.at[rows, pair]),
                    (side.at[chunk, 1], dv_ref.at[rows, pair]),
                )
            ):
                copies.append(pltpu.make_async_copy(buf, to, sem.at[chunk, i]))
                copies[-1].start()
        for c in copies:
            c.wait()


def place(facts, pack, outs):
    hbm = pl.BlockSpec(memory_space=pltpu.HBM)
    return pl.pallas_call(
        place_kernel,
        out_shape=[jax.ShapeDtypeStruct(x.shape, x.dtype) for x in outs],
        in_specs=[
            pl.BlockSpec(memory_space=pltpu.VMEM),
            pl.BlockSpec(memory_space=pltpu.VMEM),
            hbm,
            hbm,
            hbm,
            hbm,
        ],
        out_specs=[hbm] * 4,
        scratch_shapes=[
            pltpu.VMEM((2, BLOCK, PAIR), jnp.bfloat16),
            pltpu.VMEM((2, BLOCK, PAIR), jnp.bfloat16),
            pltpu.VMEM((2, 2, BLOCK, 2 * HD), jnp.bfloat16),
            pltpu.SemaphoreType.DMA((2, 4)),
        ],
        input_output_aliases={2 + i: i for i in range(4)},
        compiler_params=pltpu.CompilerParams(vmem_limit_bytes=VMEM_LIMIT),
        cost_estimate=pl.CostEstimate(
            flops=16 * GROUP * BLOCK * 2 * BLOCK * 2 * HD, bytes_accessed=2 << 20, transcendentals=0
        ),
        name="place_rows",
    )(facts, pack, *outs)


def origins(branch):
    found = []
    for chip in range(4):
        crossed = branch >> (chip & 1) & 1
        passed = chip ^ 2 * crossed
        found.append(2 * crossed ^ (branch >> 2 + passed & 1))
    return found


def body(queries, keys, values, out_grad, doc_first, doc_valid, move_plan):
    core, dp = lax.axis_size("fsdp"), lax.axis_size("dp")
    near, far = 1, core * dp // 2
    bits = (near, core, far)
    args = (queries, keys, values, out_grad)
    first, valid, plan = doc_first.T, doc_valid.T, jnp.swapaxes(move_plan, 1, 2)
    pack, branch, send, facts, *held = make_pack(bits, first, valid, plan, *args)
    other = lax.ppermute(pack, "dp", [(i, i ^ 1) for i in range(dp)])
    own = own_attention(facts, *held)

    def route(index):
        found = origins(index)

        def run(pack, other, send, facts):
            take = facts[0]
            got = []
            for step in (2, 3, 1):
                if step not in found:
                    continue
                pairs = []
                for i in range(core * dp):
                    chip = i // near % 2 + 2 * (i // far % 2)
                    if found[chip] == step:
                        pairs.append((i ^ (step & 1) * near ^ (step >> 1) * far, i))
                if step == 1:
                    pairs = sorted(set(pairs) | {(b, a) for a, b in pairs})
                sent = jnp.where(send[step - 1] == 1, other, pack)
                got.append((step, lax.ppermute(sent, ("dp", "fsdp"), pairs)))
            result = jnp.where(take == 1, other, pack)
            for step, rows in got:
                result = jnp.where(take == step + 1, rows, result)
            return result

        return run

    rows = lax.switch(branch[0], [route(i) for i in range(64)], pack, other, send, facts)
    return tuple(place(facts, rows, own))


def solution(mesh):
    rows = P(("dp", "fsdp"), None)
    return jax.shard_map(
        body,
        mesh=mesh,
        in_specs=(rows,) * 4 + (P(),) * 3,
        out_specs=(rows,) * 4,
        check_vma=False,
    )
```

```python
import functools

import jax
import jax.numpy as jnp
from jax import lax
from jax.experimental import pallas as pl
from jax.experimental.pallas import tpu as pltpu
from jax.sharding import PartitionSpec as P

HD = 128
KVH = 4
GROUP = 7
BLOCK = 64
SEQ = 2 * BLOCK
SCALE = 1.0 / HD**0.5
PAIR = 2 * GROUP * HD
TRI = GROUP * BLOCK
DIAG = 16
SIDE = 2 * BLOCK
ROWS = TRI + DIAG + 4 * SIDE
AT = TRI + DIAG
VMEM_LIMIT = 40 * 1024 * 1024

NT = (((1,), (1,)), ((), ()))
NN = (((1,), (0,)), ((), ()))
TN = (((0,), (0,)), ((), ()))


def mm(a, b, dims):
    return lax.dot_general(a, b, dims, preferred_element_type=jnp.float32)


def iota(shape, dim):
    return lax.broadcasted_iota(jnp.int32, shape, dim)


def fold_matrix():
    shape = (BLOCK, 2 * BLOCK)
    return jnp.where((iota(shape, 1) & (BLOCK - 1)) == iota(shape, 0), 1.0, 0.0).astype(jnp.bfloat16)


def turn(fold, pair):
    low = iota(pair.shape, 1) < BLOCK
    zero = jnp.zeros_like(pair)
    split = jnp.concatenate([jnp.where(low, pair, zero), jnp.where(low, zero, pair)], 0)
    return mm(fold, split, NT)


def read_moves(plan_ref, near, core, far):
    me = lax.axis_index("dp") * core + lax.axis_index("fsdp")
    base = me & ~(near + far)
    z, c = [], []
    for q in range(4):
        at = base + (q & 1) * near + (q >> 1) * far
        c.append(plan_ref[1, 1, at])
        z.append(plan_ref[0, 1, at ^ (c[q] * core)])
    y = [plan_ref[2, 1, base], plan_ref[2, 1, base + near]]
    here = ((me // near) & 1) + 2 * ((me // far) & 1)

    def pick(values, index):
        out = values[0]
        for i in range(1, len(values)):
            out = jnp.where(index == i, values[i], out)
        return out

    def origin(chip):
        crossed = pick(y, chip & 1)
        passed = chip ^ (2 * crossed)
        return pick(z, passed) ^ (2 * crossed), pick(c, passed)

    branch = y[0] + 2 * y[1] + 4 * z[0] + 8 * z[1] + 16 * z[2] + 32 * z[3]
    send = [origin(here ^ step)[1] for step in range(1, 4)]
    mine, other = origin(here)
    take = jnp.where(mine == 0, other, mine + 1)

    return branch, send, take


def fill_zeros(full):
    zero = jnp.zeros((BLOCK, HD), jnp.bfloat16)
    for h in range(GROUP):
        r = h * 2 * BLOCK
        full[r : r + BLOCK, HD:] = zero
        full[r + BLOCK : r + 2 * BLOCK, 0:HD] = zero


def fill_pair(full, rows):
    for h in range(GROUP):
        r = h * 2 * BLOCK
        full[r : r + BLOCK, 0:HD] = rows[:, h * HD : (h + 1) * HD]
        full[r + BLOCK : r + 2 * BLOCK, HD:] = rows[:, (GROUP + h) * HD : (GROUP + h + 1) * HD]


def attend(q, k, v, g, allow):
    score = jnp.where(allow, mm(k, q, NT) * SCALE, -1e30)
    weights = jnp.exp(score - jnp.max(score, axis=0, keepdims=True))
    probs = weights * (1.0 / jnp.sum(weights, axis=0, keepdims=True))
    probs_b = probs.astype(jnp.bfloat16)
    dprob = mm(v, g, NT)
    delta = jnp.sum(probs * dprob, axis=0, keepdims=True)
    dscore = (probs * (dprob - delta) * SCALE).astype(jnp.bfloat16)
    dv = mm(probs_b, g, NN).astype(jnp.bfloat16)
    dk = mm(dscore, q, NN).astype(jnp.bfloat16)
    return probs_b, dscore, dk, dv


def block_mask(live):
    wide = (BLOCK, GROUP * 2 * BLOCK)
    key_pos = iota(wide, 0)
    query_pos = iota(wide, 1) & (BLOCK - 1)
    return (key_pos <= query_pos) & (key_pos < live)


def pack_kernel(bits, first_hbm, valid_hbm, plan_hbm, q_hbm, k_hbm, v_hbm, g_hbm, *refs):
    pack_ref, send_ref, facts_ref = refs[:3]
    first_ref, valid_ref, plan_ref, qbd, gbd, sem = refs[3:9]
    bufs = refs[9:]
    q_buf, k_buf, v_buf, g_buf = bufs
    words = [
        pltpu.make_async_copy(hbm, ref, sem.at[2, i])
        for i, (hbm, ref) in enumerate(
            ((plan_hbm, plan_ref), (valid_hbm, valid_ref), (first_hbm, first_ref))
        )
    ]
    copies = []
    for chunk in range(2):
        for i, (hbm, buf) in enumerate(zip((q_hbm, k_hbm, v_hbm, g_hbm), bufs)):
            width = buf.shape[1] // 2
            cut = pl.ds(chunk * width, width)
            copies.append(
                pltpu.make_async_copy(
                    hbm.at[pl.ds(BLOCK, BLOCK), cut], buf.at[:, cut], sem.at[chunk, i]
                )
            )
    for c in words + copies:
        c.start()
    for chunk in range(2):
        fill_zeros(qbd.at[chunk])
        fill_zeros(gbd.at[chunk])
    for c in words:
        c.wait()
    branch, send, take = read_moves(plan_ref, *bits)
    me = lax.axis_index("dp") * bits[1] + lax.axis_index("fsdp")
    for i in range(3):
        send_ref[i] = jnp.full((1, HD), send[i], jnp.int32)
    facts = (take, jnp.where(first_ref[1, me] == 0, 1, 0), valid_ref[0, me], valid_ref[1, me], branch)
    for i, fact in enumerate(facts):
        facts_ref[i] = jnp.full((1, HD), fact, jnp.int32)
    allow = block_mask(valid_ref[1, me])
    fold = fold_matrix()
    square = (BLOCK, 2 * BLOCK)
    row, lane = iota(square, 0), iota(square, 1) & (BLOCK - 1)
    for c in copies:
        c.wait()
    for chunk in range(2):
        base = chunk * ROWS
        heads = slice(chunk * PAIR, (chunk + 1) * PAIR)
        pair = slice(chunk * 2 * HD, (chunk + 1) * 2 * HD)
        fill_pair(qbd.at[chunk], q_buf.at[:, heads])
        fill_pair(gbd.at[chunk], g_buf.at[:, heads])
        k, v = k_buf[:, pair], v_buf[:, pair]
        probs_b, dscore, dk, dv = attend(qbd[chunk], k, v, gbd[chunk], allow)
        diag = []
        for h in range(GROUP):
            cut = slice(h * 2 * BLOCK, (h + 1) * 2 * BLOCK)
            ds = dscore[:, cut]
            pack_ref[base + h * BLOCK : base + (h + 1) * BLOCK, :] = jnp.where(
                row <= lane, probs_b[:, cut].astype(jnp.float32), turn(fold, ds)
            ).astype(jnp.bfloat16)
            diag.append(
                jnp.sum(jnp.where(row == lane, ds.astype(jnp.float32), 0.0), axis=0, keepdims=True)
            )
        diag.append(jnp.zeros((DIAG - GROUP, 2 * BLOCK), jnp.float32))
        pack_ref[base + TRI : base + AT, :] = jnp.concatenate(diag, 0).astype(jnp.bfloat16)
        for i, part in enumerate((k, v, dk, dv)):
            for j in range(2):
                r = base + AT + i * SIDE + j * BLOCK
                pack_ref[r : r + BLOCK, :] = part[:, j * HD : (j + 1) * HD]


def make_pack(bits, first, valid, plan, q, k, v, g):
    hbm = pl.BlockSpec(memory_space=pltpu.HBM)
    vmem = pl.BlockSpec(memory_space=pltpu.VMEM)
    return pl.pallas_call(
        functools.partial(pack_kernel, bits),
        out_shape=[
            pltpu.VMEM((2 * ROWS, HD), jnp.bfloat16),
            pltpu.VMEM((3, 1, HD), jnp.int32),
            pltpu.VMEM((5, 1, HD), jnp.int32),
        ],
        in_specs=[hbm] * 7,
        out_specs=[vmem] * 3,
        scratch_shapes=[
            pltpu.SMEM(first.shape, jnp.int32),
            pltpu.SMEM(valid.shape, jnp.int32),
            pltpu.SMEM(plan.shape, jnp.int32),
            pltpu.VMEM((2, GROUP * 2 * BLOCK, 2 * HD), jnp.bfloat16),
            pltpu.VMEM((2, GROUP * 2 * BLOCK, 2 * HD), jnp.bfloat16),
            pltpu.SemaphoreType.DMA((3, 4)),
        ]
        + [pltpu.VMEM((BLOCK, x.shape[1]), x.dtype) for x in (q, k, v, g)],
        compiler_params=pltpu.CompilerParams(vmem_limit_bytes=VMEM_LIMIT),
        cost_estimate=pl.CostEstimate(
            flops=16 * BLOCK * GROUP * 2 * BLOCK * 2 * HD, bytes_accessed=3 << 20, transcendentals=0
        ),
        name="pack_rows",
    )(*(pltpu.with_memory_space_constraint(x, pltpu.HBM) for x in (first, valid, plan, q, k, v, g)))


def finish_kernel(facts_ref, pack, q_hbm, k_hbm, v_hbm, g_hbm, *refs):
    outs, ins, news = refs[:4], refs[4:8], refs[8:12]
    qbd, gbd, in_sem, out_sem = refs[12:]
    q_buf, k_buf, v_buf, g_buf = ins
    o_buf, dq_buf, dk_buf, dv_buf = news
    joined = jnp.max(facts_ref[1]) == 1

    def read(block):
        rows = pl.ds(block * BLOCK, BLOCK)
        return [
            pltpu.make_async_copy(hbm.at[rows, :], buf.at[rows, :], in_sem.at[block, i])
            for i, (hbm, buf) in enumerate(zip((q_hbm, k_hbm, v_hbm, g_hbm), ins))
        ]

    def write(block, part, parts):
        copies = []
        for i, (buf, out) in enumerate(zip(news, outs)):
            width = buf.shape[1] // parts
            at = (pl.ds(block * BLOCK, BLOCK), pl.ds(part * width, width))
            copies.append(
                pltpu.make_async_copy(buf.at[at], out.at[at], out_sem.at[2 * block + part, i])
            )
            copies[-1].start()
        return copies

    low, high = read(0), read(1)
    for c in low:
        c.start()

    @pl.when(joined)
    def _():
        for c in high:
            c.start()

    @pl.when(jnp.logical_not(joined))
    def _():
        fold = fold_matrix()
        square = (BLOCK, 2 * BLOCK)
        row, lane = iota(square, 0), iota(square, 1) & (BLOCK - 1)
        zero = jnp.zeros((BLOCK, HD), jnp.bfloat16)
        copies = []
        for chunk in range(2):
            fill_zeros(qbd.at[chunk])
            fill_zeros(gbd.at[chunk])
        for chunk in range(2):
            base = chunk * ROWS

            def spread(i):
                r = base + AT + i * SIDE
                return jnp.concatenate(
                    [
                        jnp.concatenate([pack[r : r + BLOCK, :], zero], 1),
                        jnp.concatenate([zero, pack[r + BLOCK : r + SIDE, :]], 1),
                    ],
                    0,
                )

            kbd, vbd = spread(0), spread(1)
            for j in range(2):
                for i, buf in ((2, dk_buf), (3, dv_buf)):
                    r, at = base + AT + i * SIDE + j * BLOCK, (2 * chunk + j) * HD
                    buf[BLOCK:, at : at + HD] = pack[r : r + BLOCK, :]
            diag = pack[base + TRI : base + AT, :].astype(jnp.float32)
            probs, dscore = [], []
            for h in range(GROUP):
                both = pack[base + h * BLOCK : base + (h + 1) * BLOCK, :].astype(jnp.float32)
                upper = jnp.where(row <= lane, both, 0.0).astype(jnp.bfloat16)
                probs.append(turn(fold, upper).astype(jnp.bfloat16))
                line = jnp.where(row == lane, diag[h : h + 1, :], 0.0)
                dscore.append(jnp.where(row > lane, both, line).astype(jnp.bfloat16))
            out = mm(jnp.concatenate(probs, 0), vbd, NN).astype(jnp.bfloat16)
            dq = mm(jnp.concatenate(dscore, 0), kbd, NN).astype(jnp.bfloat16)
            for buf, val in ((o_buf, out), (dq_buf, dq)):
                for h in range(GROUP):
                    for j in range(2):
                        at = chunk * PAIR + (j * GROUP + h) * HD
                        buf[BLOCK:, at : at + HD] = val[
                            h * BLOCK : (h + 1) * BLOCK, j * HD : (j + 1) * HD
                        ]
        copies += write(1, 0, 1)
        for c in low:
            c.wait()
        allow = block_mask(jnp.max(facts_ref[2]))
        for chunk in range(2):
            heads = slice(chunk * PAIR, (chunk + 1) * PAIR)
            pair = slice(chunk * 2 * HD, (chunk + 1) * 2 * HD)
            fill_pair(qbd.at[chunk], q_buf.at[0:BLOCK, heads])
            fill_pair(gbd.at[chunk], g_buf.at[0:BLOCK, heads])
            k, v = k_buf[0:BLOCK, pair], v_buf[0:BLOCK, pair]
            probs_b, dscore, dk, dv = attend(qbd[chunk], k, v, gbd[chunk], allow)
            dk_buf[0:BLOCK, pair] = dk
            dv_buf[0:BLOCK, pair] = dv
            for buf, squares, other in ((o_buf, probs_b, v), (dq_buf, dscore, k)):
                val = mm(squares, other, TN).astype(jnp.bfloat16)
                for h in range(GROUP):
                    for j in range(2):
                        r, at = (2 * h + j) * BLOCK, chunk * PAIR + (j * GROUP + h) * HD
                        buf[0:BLOCK, at : at + HD] = val[r : r + BLOCK, j * HD : (j + 1) * HD]
            copies += write(0, chunk, 2)
        for c in copies:
            c.wait()

    @pl.when(joined)
    def _():
        for c in low + high:
            c.wait()
        wide = (SEQ, GROUP * SEQ)
        key_pos = iota(wide, 0)
        query_pos = iota(wide, 1) & (SEQ - 1)
        live_of = jnp.where(key_pos < BLOCK, jnp.max(facts_ref[2]), jnp.max(facts_ref[3]))
        allow = (key_pos <= query_pos) & ((key_pos & (BLOCK - 1)) < live_of)

        @pl.loop(0, KVH)
        def _(i):
            one = pl.ds(pl.multiple_of(i * HD, HD), HD)

            def head(h):
                return pl.ds(pl.multiple_of((i * GROUP + h) * HD, HD), HD)

            k, v = k_buf[:, one], v_buf[:, one]
            q = jnp.concatenate([q_buf[:, head(h)] for h in range(GROUP)], 0)
            g = jnp.concatenate([g_buf[:, head(h)] for h in range(GROUP)], 0)
            probs_b, dscore, dk, dv = attend(q, k, v, g, allow)
            dk_buf[:, one] = dk
            dv_buf[:, one] = dv
            for h in range(GROUP):
                cut = slice(h * SEQ, (h + 1) * SEQ)
                o_buf[:, head(h)] = mm(probs_b[:, cut], v, TN).astype(jnp.bfloat16)
                dq_buf[:, head(h)] = mm(dscore[:, cut], k, TN).astype(jnp.bfloat16)

        for c in write(0, 0, 1) + write(1, 0, 1):
            c.wait()


def finish(facts, pack, q, k, v, g):
    vmem = pl.BlockSpec(memory_space=pltpu.VMEM)
    hbm = pl.BlockSpec(memory_space=pltpu.HBM)
    return pl.pallas_call(
        finish_kernel,
        out_shape=[jax.ShapeDtypeStruct(x.shape, jnp.bfloat16) for x in (q, q, k, v)],
        in_specs=[vmem] * 2 + [hbm] * 4,
        out_specs=[hbm] * 4,
        scratch_shapes=[pltpu.VMEM(x.shape, jnp.bfloat16) for x in (q, k, v, g, q, q, k, v)]
        + [pltpu.VMEM((2, GROUP * 2 * BLOCK, 2 * HD), jnp.bfloat16)] * 2
        + [pltpu.SemaphoreType.DMA((2, 4)), pltpu.SemaphoreType.DMA((4, 4))],
        compiler_params=pltpu.CompilerParams(vmem_limit_bytes=VMEM_LIMIT),
        cost_estimate=pl.CostEstimate(
            flops=12 * KVH * GROUP * SEQ * SEQ * HD, bytes_accessed=4 << 20, transcendentals=0
        ),
        name="finish_rows",
    )(facts, pack, *(pltpu.with_memory_space_constraint(x, pltpu.HBM) for x in (q, k, v, g)))


def origins(branch):
    found = []
    for chip in range(4):
        crossed = branch >> (chip & 1) & 1
        passed = chip ^ 2 * crossed
        found.append(2 * crossed ^ (branch >> 2 + passed & 1))
    return found


def body(queries, keys, values, out_grad, doc_first, doc_valid, move_plan):
    core, dp = lax.axis_size("fsdp"), lax.axis_size("dp")
    near, far = 1, core * dp // 2
    bits = (near, core, far)
    args = (queries, keys, values, out_grad)
    first, valid, plan = doc_first.T, doc_valid.T, jnp.swapaxes(move_plan, 1, 2)
    pack, send, facts = make_pack(bits, first, valid, plan, *args)
    other = lax.ppermute(pack, "dp", [(i, i ^ 1) for i in range(dp)])

    def route(index):
        found = origins(index)

        def run(pack, other, send, facts):
            take = facts[0]
            got = []
            for step in (1, 2, 3):
                if step not in found:
                    continue
                chips = [chip for chip in range(4) if found[chip] == step]
                if len(chips) == 3:
                    chips = [0, 1, 2, 3]
                pairs = []
                for i in range(core * dp):
                    if i // near % 2 + 2 * (i // far % 2) in chips:
                        pairs.append((i ^ (step & 1) * near ^ (step >> 1) * far, i))
                sent = jnp.where(send[step - 1] == 1, other, pack)
                got.append((step, lax.ppermute(sent, ("dp", "fsdp"), pairs)))
            result = jnp.where(take == 1, other, pack)
            for step, rows in got:
                result = jnp.where(take == step + 1, rows, result)
            return result

        return run

    rows = lax.switch(facts[4, 0, 0], [route(i) for i in range(64)], pack, other, send, facts)
    return tuple(finish(facts, rows, *args))


def solution(mesh):
    rows = P(("dp", "fsdp"), None)
    return jax.shard_map(
        body,
        mesh=mesh,
        in_specs=(rows,) * 4 + (P(),) * 3,
        out_specs=(rows,) * 4,
        check_vma=False,
    )
```

```python
import functools

import jax
import jax.numpy as jnp
from jax import lax
from jax.experimental import pallas as pl
from jax.experimental.pallas import tpu as pltpu
from jax.sharding import PartitionSpec as P

HD = 128
KVH = 4
GROUP = 7
BLOCK = 64
SEQ = 2 * BLOCK
SCALE = 1.0 / HD**0.5
PAIR = 2 * GROUP * HD
TRI = GROUP * BLOCK
DIAG = 16
SIDE = 2 * BLOCK
ROWS = TRI + DIAG + 4 * SIDE
AT = TRI + DIAG
VMEM_LIMIT = 40 * 1024 * 1024

NT = (((1,), (1,)), ((), ()))
NN = (((1,), (0,)), ((), ()))
TN = (((0,), (0,)), ((), ()))


def mm(a, b, dims):
    return lax.dot_general(a, b, dims, preferred_element_type=jnp.float32)


def iota(shape, dim):
    return lax.broadcasted_iota(jnp.int32, shape, dim)


def fold_matrix():
    shape = (BLOCK, 2 * BLOCK)
    return jnp.where((iota(shape, 1) & (BLOCK - 1)) == iota(shape, 0), 1.0, 0.0).astype(jnp.bfloat16)


def turn(fold, pair):
    low = iota(pair.shape, 1) < BLOCK
    zero = jnp.zeros_like(pair)
    split = jnp.concatenate([jnp.where(low, pair, zero), jnp.where(low, zero, pair)], 0)
    return mm(fold, split, NT)


def read_moves(plan_ref, near, core, far):
    me = lax.axis_index("dp") * core + lax.axis_index("fsdp")
    base = me & ~(near + far)
    z, c = [], []
    for q in range(4):
        at = base + (q & 1) * near + (q >> 1) * far
        c.append(plan_ref[1, 1, at])
        z.append(plan_ref[0, 1, at ^ (c[q] * core)])
    y = [plan_ref[2, 1, base], plan_ref[2, 1, base + near]]
    here = ((me // near) & 1) + 2 * ((me // far) & 1)

    def pick(values, index):
        out = values[0]
        for i in range(1, len(values)):
            out = jnp.where(index == i, values[i], out)
        return out

    def origin(chip):
        crossed = pick(y, chip & 1)
        passed = chip ^ (2 * crossed)
        return pick(z, passed) ^ (2 * crossed), pick(c, passed)

    branch = y[0] + 2 * y[1] + 4 * z[0] + 8 * z[1] + 16 * z[2] + 32 * z[3]
    send = [origin(here ^ step)[1] for step in range(1, 4)]
    mine, other = origin(here)
    take = jnp.where(mine == 0, other, mine + 1)

    return branch, send, take


def fill_zeros(full):
    zero = jnp.zeros((BLOCK, HD), jnp.bfloat16)
    for h in range(GROUP):
        r = h * 2 * BLOCK
        full[r : r + BLOCK, HD:] = zero
        full[r + BLOCK : r + 2 * BLOCK, 0:HD] = zero


def fill_pair(full, rows):
    for h in range(GROUP):
        r = h * 2 * BLOCK
        full[r : r + BLOCK, 0:HD] = rows[:, h * HD : (h + 1) * HD]
        full[r + BLOCK : r + 2 * BLOCK, HD:] = rows[:, (GROUP + h) * HD : (GROUP + h + 1) * HD]


def attend(q, k, v, g, allow):
    score = jnp.where(allow, mm(k, q, NT) * SCALE, -1e30)
    weights = jnp.exp(score - jnp.max(score, axis=0, keepdims=True))
    probs = weights * (1.0 / jnp.sum(weights, axis=0, keepdims=True))
    probs_b = probs.astype(jnp.bfloat16)
    dprob = mm(v, g, NT)
    delta = jnp.sum(probs * dprob, axis=0, keepdims=True)
    dscore = (probs * (dprob - delta) * SCALE).astype(jnp.bfloat16)
    dv = mm(probs_b, g, NN).astype(jnp.bfloat16)
    dk = mm(dscore, q, NN).astype(jnp.bfloat16)
    return probs_b, dscore, dk, dv


def block_mask(live):
    wide = (BLOCK, GROUP * 2 * BLOCK)
    key_pos = iota(wide, 0)
    query_pos = iota(wide, 1) & (BLOCK - 1)
    return (key_pos <= query_pos) & (key_pos < live)


def pack_kernel(bits, first_hbm, valid_hbm, plan_hbm, q_hbm, k_hbm, v_hbm, g_hbm, *refs):
    pack_ref, send_ref, facts_ref = refs[:3]
    first_ref, valid_ref, plan_ref, qbd, gbd, sem = refs[3:9]
    bufs = refs[9:]
    q_buf, k_buf, v_buf, g_buf = bufs
    words = [
        pltpu.make_async_copy(hbm, ref, sem.at[2, i])
        for i, (hbm, ref) in enumerate(
            ((plan_hbm, plan_ref), (valid_hbm, valid_ref), (first_hbm, first_ref))
        )
    ]
    copies = []
    for chunk in range(2):
        for i, (hbm, buf) in enumerate(zip((q_hbm, k_hbm, v_hbm, g_hbm), bufs)):
            width = buf.shape[1] // 2
            cut = pl.ds(chunk * width, width)
            copies.append(
                pltpu.make_async_copy(
                    hbm.at[pl.ds(BLOCK, BLOCK), cut], buf.at[:, cut], sem.at[chunk, i]
                )
            )
    for c in words + copies:
        c.start()
    for chunk in range(2):
        fill_zeros(qbd.at[chunk])
        fill_zeros(gbd.at[chunk])
    for c in words:
        c.wait()
    branch, send, take = read_moves(plan_ref, *bits)
    me = lax.axis_index("dp") * bits[1] + lax.axis_index("fsdp")
    for i in range(3):
        send_ref[i] = jnp.full((1, HD), send[i], jnp.int32)
    facts = (take, jnp.where(first_ref[1, me] == 0, 1, 0), valid_ref[0, me], valid_ref[1, me], branch)
    for i, fact in enumerate(facts):
        facts_ref[i] = jnp.full((1, HD), fact, jnp.int32)
    allow = block_mask(valid_ref[1, me])
    fold = fold_matrix()
    square = (BLOCK, 2 * BLOCK)
    row, lane = iota(square, 0), iota(square, 1) & (BLOCK - 1)
    for chunk in range(2):
        for c in copies[4 * chunk : 4 * chunk + 4]:
            c.wait()
        base = chunk * ROWS
        heads = slice(chunk * PAIR, (chunk + 1) * PAIR)
        pair = slice(chunk * 2 * HD, (chunk + 1) * 2 * HD)
        fill_pair(qbd.at[chunk], q_buf.at[:, heads])
        fill_pair(gbd.at[chunk], g_buf.at[:, heads])
        k, v = k_buf[:, pair], v_buf[:, pair]
        probs_b, dscore, dk, dv = attend(qbd[chunk], k, v, gbd[chunk], allow)
        diag = []
        for h in range(GROUP):
            cut = slice(h * 2 * BLOCK, (h + 1) * 2 * BLOCK)
            ds = dscore[:, cut]
            pack_ref[base + h * BLOCK : base + (h + 1) * BLOCK, :] = jnp.where(
                row <= lane, probs_b[:, cut].astype(jnp.float32), turn(fold, ds)
            ).astype(jnp.bfloat16)
            diag.append(
                jnp.sum(jnp.where(row == lane, ds.astype(jnp.float32), 0.0), axis=0, keepdims=True)
            )
        diag.append(jnp.zeros((DIAG - GROUP, 2 * BLOCK), jnp.float32))
        pack_ref[base + TRI : base + AT, :] = jnp.concatenate(diag, 0).astype(jnp.bfloat16)
        for i, part in enumerate((k, v, dk, dv)):
            for j in range(2):
                r = base + AT + i * SIDE + j * BLOCK
                pack_ref[r : r + BLOCK, :] = part[:, j * HD : (j + 1) * HD]


def make_pack(bits, first, valid, plan, q, k, v, g):
    hbm = pl.BlockSpec(memory_space=pltpu.HBM)
    vmem = pl.BlockSpec(memory_space=pltpu.VMEM)
    return pl.pallas_call(
        functools.partial(pack_kernel, bits),
        out_shape=[
            pltpu.VMEM((2 * ROWS, HD), jnp.bfloat16),
            pltpu.VMEM((3, 1, HD), jnp.int32),
            pltpu.VMEM((5, 1, HD), jnp.int32),
        ],
        in_specs=[hbm] * 7,
        out_specs=[vmem] * 3,
        scratch_shapes=[
            pltpu.SMEM(first.shape, jnp.int32),
            pltpu.SMEM(valid.shape, jnp.int32),
            pltpu.SMEM(plan.shape, jnp.int32),
            pltpu.VMEM((2, GROUP * 2 * BLOCK, 2 * HD), jnp.bfloat16),
            pltpu.VMEM((2, GROUP * 2 * BLOCK, 2 * HD), jnp.bfloat16),
            pltpu.SemaphoreType.DMA((3, 4)),
        ]
        + [pltpu.VMEM((BLOCK, x.shape[1]), x.dtype) for x in (q, k, v, g)],
        compiler_params=pltpu.CompilerParams(vmem_limit_bytes=VMEM_LIMIT),
        cost_estimate=pl.CostEstimate(
            flops=16 * BLOCK * GROUP * 2 * BLOCK * 2 * HD, bytes_accessed=3 << 20, transcendentals=0
        ),
        name="pack_rows",
    )(*(pltpu.with_memory_space_constraint(x, pltpu.HBM) for x in (first, valid, plan, q, k, v, g)))


def finish_kernel(facts_ref, pack, q_hbm, k_hbm, v_hbm, g_hbm, *refs):
    outs, ins, news = refs[:4], refs[4:8], refs[8:12]
    qbd, gbd, in_sem, out_sem = refs[12:]
    q_buf, k_buf, v_buf, g_buf = ins
    o_buf, dq_buf, dk_buf, dv_buf = news
    joined = jnp.max(facts_ref[1]) == 1

    def read(block):
        rows = pl.ds(block * BLOCK, BLOCK)
        return [
            pltpu.make_async_copy(hbm.at[rows, :], buf.at[rows, :], in_sem.at[block, i])
            for i, (hbm, buf) in enumerate(zip((q_hbm, k_hbm, v_hbm, g_hbm), ins))
        ]

    def write(block, part, parts):
        copies = []
        for i, (buf, out) in enumerate(zip(news, outs)):
            width = buf.shape[1] // parts
            at = (pl.ds(block * BLOCK, BLOCK), pl.ds(part * width, width))
            copies.append(
                pltpu.make_async_copy(buf.at[at], out.at[at], out_sem.at[2 * block + part, i])
            )
            copies[-1].start()
        return copies

    low, high = read(0), read(1)
    for c in low:
        c.start()

    @pl.when(joined)
    def _():
        for c in high:
            c.start()

    @pl.when(jnp.logical_not(joined))
    def _():
        fold = fold_matrix()
        square = (BLOCK, 2 * BLOCK)
        row, lane = iota(square, 0), iota(square, 1) & (BLOCK - 1)
        zero = jnp.zeros((BLOCK, HD), jnp.bfloat16)
        copies = []
        for chunk in range(2):
            fill_zeros(qbd.at[chunk])
            fill_zeros(gbd.at[chunk])
        for chunk in range(2):
            base = chunk * ROWS

            def spread(i):
                r = base + AT + i * SIDE
                return jnp.concatenate(
                    [
                        jnp.concatenate([pack[r : r + BLOCK, :], zero], 1),
                        jnp.concatenate([zero, pack[r + BLOCK : r + SIDE, :]], 1),
                    ],
                    0,
                )

            kbd, vbd = spread(0), spread(1)
            for j in range(2):
                for i, buf in ((2, dk_buf), (3, dv_buf)):
                    r, at = base + AT + i * SIDE + j * BLOCK, (2 * chunk + j) * HD
                    buf[BLOCK:, at : at + HD] = pack[r : r + BLOCK, :]
            diag = pack[base + TRI : base + AT, :].astype(jnp.float32)
            probs, dscore = [], []
            for h in range(GROUP):
                both = pack[base + h * BLOCK : base + (h + 1) * BLOCK, :].astype(jnp.float32)
                upper = jnp.where(row <= lane, both, 0.0).astype(jnp.bfloat16)
                probs.append(turn(fold, upper).astype(jnp.bfloat16))
                line = jnp.where(row == lane, diag[h : h + 1, :], 0.0)
                dscore.append(jnp.where(row > lane, both, line).astype(jnp.bfloat16))
            out = mm(jnp.concatenate(probs, 0), vbd, NN).astype(jnp.bfloat16)
            dq = mm(jnp.concatenate(dscore, 0), kbd, NN).astype(jnp.bfloat16)
            for buf, val in ((o_buf, out), (dq_buf, dq)):
                for h in range(GROUP):
                    for j in range(2):
                        at = chunk * PAIR + (j * GROUP + h) * HD
                        buf[BLOCK:, at : at + HD] = val[
                            h * BLOCK : (h + 1) * BLOCK, j * HD : (j + 1) * HD
                        ]
            copies += write(1, chunk, 2)
        for c in low:
            c.wait()
        allow = block_mask(jnp.max(facts_ref[2]))
        for chunk in range(2):
            heads = slice(chunk * PAIR, (chunk + 1) * PAIR)
            pair = slice(chunk * 2 * HD, (chunk + 1) * 2 * HD)
            fill_pair(qbd.at[chunk], q_buf.at[0:BLOCK, heads])
            fill_pair(gbd.at[chunk], g_buf.at[0:BLOCK, heads])
            k, v = k_buf[0:BLOCK, pair], v_buf[0:BLOCK, pair]
            probs_b, dscore, dk, dv = attend(qbd[chunk], k, v, gbd[chunk], allow)
            dk_buf[0:BLOCK, pair] = dk
            dv_buf[0:BLOCK, pair] = dv
            for buf, squares, other in ((o_buf, probs_b, v), (dq_buf, dscore, k)):
                turned = squares.T
                for j in range(2):
                    rows = [turned[(2 * h + j) * BLOCK : (2 * h + j + 1) * BLOCK] for h in range(GROUP)]
                    val = mm(jnp.concatenate(rows, 0), other[:, j * HD : (j + 1) * HD], NN).astype(jnp.bfloat16)
                    for h in range(GROUP):
                        at = chunk * PAIR + (j * GROUP + h) * HD
                        buf[0:BLOCK, at : at + HD] = val[h * BLOCK : (h + 1) * BLOCK]
            copies += write(0, chunk, 2)
        for c in copies:
            c.wait()

    @pl.when(joined)
    def _():
        for c in low + high:
            c.wait()
        wide = (SEQ, GROUP * SEQ)
        key_pos = iota(wide, 0)
        query_pos = iota(wide, 1) & (SEQ - 1)
        live_of = jnp.where(key_pos < BLOCK, jnp.max(facts_ref[2]), jnp.max(facts_ref[3]))
        allow = (key_pos <= query_pos) & ((key_pos & (BLOCK - 1)) < live_of)

        @pl.loop(0, KVH)
        def _(i):
            one = pl.ds(pl.multiple_of(i * HD, HD), HD)

            def head(h):
                return pl.ds(pl.multiple_of((i * GROUP + h) * HD, HD), HD)

            k, v = k_buf[:, one], v_buf[:, one]
            q = jnp.concatenate([q_buf[:, head(h)] for h in range(GROUP)], 0)
            g = jnp.concatenate([g_buf[:, head(h)] for h in range(GROUP)], 0)
            probs_b, dscore, dk, dv = attend(q, k, v, g, allow)
            dk_buf[:, one] = dk
            dv_buf[:, one] = dv
            for h in range(GROUP):
                cut = slice(h * SEQ, (h + 1) * SEQ)
                o_buf[:, head(h)] = mm(probs_b[:, cut], v, TN).astype(jnp.bfloat16)
                dq_buf[:, head(h)] = mm(dscore[:, cut], k, TN).astype(jnp.bfloat16)

        for c in write(0, 0, 1) + write(1, 0, 1):
            c.wait()


def finish(facts, pack, q, k, v, g):
    vmem = pl.BlockSpec(memory_space=pltpu.VMEM)
    hbm = pl.BlockSpec(memory_space=pltpu.HBM)
    return pl.pallas_call(
        finish_kernel,
        out_shape=[jax.ShapeDtypeStruct(x.shape, jnp.bfloat16) for x in (q, q, k, v)],
        in_specs=[vmem] * 2 + [hbm] * 4,
        out_specs=[hbm] * 4,
        scratch_shapes=[pltpu.VMEM(x.shape, jnp.bfloat16) for x in (q, k, v, g, q, q, k, v)]
        + [pltpu.VMEM((2, GROUP * 2 * BLOCK, 2 * HD), jnp.bfloat16)] * 2
        + [pltpu.SemaphoreType.DMA((2, 4)), pltpu.SemaphoreType.DMA((4, 4))],
        compiler_params=pltpu.CompilerParams(vmem_limit_bytes=VMEM_LIMIT),
        cost_estimate=pl.CostEstimate(
            flops=12 * KVH * GROUP * SEQ * SEQ * HD, bytes_accessed=4 << 20, transcendentals=0
        ),
        name="finish_rows",
    )(facts, pack, *(pltpu.with_memory_space_constraint(x, pltpu.HBM) for x in (q, k, v, g)))


def origins(branch):
    found = []
    for chip in range(4):
        crossed = branch >> (chip & 1) & 1
        passed = chip ^ 2 * crossed
        found.append(2 * crossed ^ (branch >> 2 + passed & 1))
    return found


def body(queries, keys, values, out_grad, doc_first, doc_valid, move_plan):
    core, dp = lax.axis_size("fsdp"), lax.axis_size("dp")
    near, far = 1, core * dp // 2
    bits = (near, core, far)
    args = (queries, keys, values, out_grad)
    first, valid, plan = doc_first.T, doc_valid.T, jnp.swapaxes(move_plan, 1, 2)
    pack, send, facts = make_pack(bits, first, valid, plan, *args)
    other = lax.ppermute(pack, "dp", [(i, i ^ 1) for i in range(dp)])

    def route(index):
        found = origins(index)

        def run(pack, other, send, facts):
            take = facts[0]
            got = []
            for step in (1, 2, 3):
                if step not in found:
                    continue
                chips = [chip for chip in range(4) if found[chip] == step]
                if len(chips) == 3:
                    chips = [0, 1, 2, 3]
                pairs = []
                for i in range(core * dp):
                    if i // near % 2 + 2 * (i // far % 2) in chips:
                        pairs.append((i ^ (step & 1) * near ^ (step >> 1) * far, i))
                sent = jnp.where(send[step - 1] == 1, other, pack)
                got.append((step, lax.ppermute(sent, ("dp", "fsdp"), pairs)))
            result = jnp.where(take == 1, other, pack)
            for step, rows in got:
                result = jnp.where(take == step + 1, rows, result)
            return result

        return run

    rows = lax.switch(facts[4, 0, 0], [route(i) for i in range(64)], pack, other, send, facts)
    return tuple(finish(facts, rows, *args))


def solution(mesh):
    rows = P(("dp", "fsdp"), None)
    return jax.shard_map(
        body,
        mesh=mesh,
        in_specs=(rows,) * 4 + (P(),) * 3,
        out_specs=(rows,) * 4,
        check_vma=False,
    )
```

```python
import functools

import jax
import jax.numpy as jnp
from jax import lax
from jax.experimental import pallas as pl
from jax.experimental.pallas import tpu as pltpu
from jax.sharding import PartitionSpec as P

HD = 128
KVH = 4
GROUP = 7
BLOCK = 64
SEQ = 2 * BLOCK
SCALE = 1.0 / HD**0.5
PAIR = 2 * GROUP * HD
TRI = GROUP * BLOCK
DIAG = 16
SIDE = 2 * BLOCK
ROWS = TRI + 4 * SIDE
AT = TRI
VMEM_LIMIT = 40 * 1024 * 1024

NT = (((1,), (1,)), ((), ()))
NN = (((1,), (0,)), ((), ()))
TN = (((0,), (0,)), ((), ()))


def mm(a, b, dims):
    return lax.dot_general(a, b, dims, preferred_element_type=jnp.float32)


def iota(shape, dim):
    return lax.broadcasted_iota(jnp.int32, shape, dim)


def fold_matrix():
    shape = (BLOCK, 2 * BLOCK)
    return jnp.where((iota(shape, 1) & (BLOCK - 1)) == iota(shape, 0), 1.0, 0.0).astype(jnp.bfloat16)


def turn(fold, pair):
    low = iota(pair.shape, 1) < BLOCK
    zero = jnp.zeros_like(pair)
    split = jnp.concatenate([jnp.where(low, pair, zero), jnp.where(low, zero, pair)], 0)
    return mm(fold, split, NT)


def read_moves(plan_ref, near, core, far):
    me = lax.axis_index("dp") * core + lax.axis_index("fsdp")
    base = me & ~(near + far)
    z, c = [], []
    for q in range(4):
        at = base + (q & 1) * near + (q >> 1) * far
        c.append(plan_ref[1, 1, at])
        z.append(plan_ref[0, 1, at ^ (c[q] * core)])
    y = [plan_ref[2, 1, base], plan_ref[2, 1, base + near]]
    here = ((me // near) & 1) + 2 * ((me // far) & 1)

    def pick(values, index):
        out = values[0]
        for i in range(1, len(values)):
            out = jnp.where(index == i, values[i], out)
        return out

    def origin(chip):
        crossed = pick(y, chip & 1)
        passed = chip ^ (2 * crossed)
        return pick(z, passed) ^ (2 * crossed), pick(c, passed)

    branch = y[0] + 2 * y[1] + 4 * z[0] + 8 * z[1] + 16 * z[2] + 32 * z[3]
    send = [origin(here ^ step)[1] for step in range(1, 4)]
    mine, other = origin(here)
    take = jnp.where(mine == 0, other, mine + 1)

    return branch, send, take


def fill_zeros(full):
    zero = jnp.zeros((BLOCK, HD), jnp.bfloat16)
    for h in range(GROUP):
        r = h * 2 * BLOCK
        full[r : r + BLOCK, HD:] = zero
        full[r + BLOCK : r + 2 * BLOCK, 0:HD] = zero


def fill_pair(full, rows):
    for h in range(GROUP):
        r = h * 2 * BLOCK
        full[r : r + BLOCK, 0:HD] = rows[:, h * HD : (h + 1) * HD]
        full[r + BLOCK : r + 2 * BLOCK, HD:] = rows[:, (GROUP + h) * HD : (GROUP + h + 1) * HD]


def attend(q, k, v, g, allow):
    score = jnp.where(allow, mm(k, q, NT) * SCALE, -1e30)
    weights = jnp.exp(score - jnp.max(score, axis=0, keepdims=True))
    probs = weights * (1.0 / jnp.sum(weights, axis=0, keepdims=True))
    probs_b = probs.astype(jnp.bfloat16)
    dprob = mm(v, g, NT)
    delta = jnp.sum(probs * dprob, axis=0, keepdims=True)
    dscore = (probs * (dprob - delta) * SCALE).astype(jnp.bfloat16)
    dv = mm(probs_b, g, NN).astype(jnp.bfloat16)
    dk = mm(dscore, q, NN).astype(jnp.bfloat16)
    return probs_b, dscore, dk, dv


def block_mask(live):
    wide = (BLOCK, GROUP * 2 * BLOCK)
    key_pos = iota(wide, 0)
    query_pos = iota(wide, 1) & (BLOCK - 1)
    return (key_pos <= query_pos) & (key_pos < live)


def pack_kernel(bits, first_hbm, valid_hbm, plan_hbm, q_hbm, k_hbm, v_hbm, g_hbm, *refs):
    pack_ref, send_ref, facts_ref = refs[:3]
    first_ref, valid_ref, plan_ref, qbd, gbd, sem = refs[3:9]
    bufs = refs[9:]
    q_buf, k_buf, v_buf, g_buf = bufs
    words = [
        pltpu.make_async_copy(hbm, ref, sem.at[2, i])
        for i, (hbm, ref) in enumerate(
            ((plan_hbm, plan_ref), (valid_hbm, valid_ref), (first_hbm, first_ref))
        )
    ]
    copies = []
    for chunk in range(2):
        for i, (hbm, buf) in enumerate(zip((q_hbm, k_hbm, v_hbm, g_hbm), bufs)):
            width = buf.shape[1] // 2
            cut = pl.ds(chunk * width, width)
            copies.append(
                pltpu.make_async_copy(
                    hbm.at[pl.ds(BLOCK, BLOCK), cut], buf.at[:, cut], sem.at[chunk, i]
                )
            )
    for c in words + copies:
        c.start()
    for chunk in range(2):
        fill_zeros(qbd.at[chunk])
        fill_zeros(gbd.at[chunk])
    for c in words:
        c.wait()
    branch, send, take = read_moves(plan_ref, *bits)
    me = lax.axis_index("dp") * bits[1] + lax.axis_index("fsdp")
    for i in range(3):
        send_ref[i] = jnp.full((1, HD), send[i], jnp.int32)
    facts = (take, jnp.where(first_ref[1, me] == 0, 1, 0), valid_ref[0, me], valid_ref[1, me], branch)
    for i, fact in enumerate(facts):
        facts_ref[i] = jnp.full((1, HD), fact, jnp.int32)
    allow = block_mask(valid_ref[1, me])
    fold = fold_matrix()
    square = (BLOCK, 2 * BLOCK)
    row, lane = iota(square, 0), iota(square, 1) & (BLOCK - 1)
    diag = []
    for chunk in range(2):
        for c in copies[4 * chunk : 4 * chunk + 4]:
            c.wait()
        base = chunk * ROWS
        heads = slice(chunk * PAIR, (chunk + 1) * PAIR)
        pair = slice(chunk * 2 * HD, (chunk + 1) * 2 * HD)
        fill_pair(qbd.at[chunk], q_buf.at[:, heads])
        fill_pair(gbd.at[chunk], g_buf.at[:, heads])
        k, v = k_buf[:, pair], v_buf[:, pair]
        probs_b, dscore, dk, dv = attend(qbd[chunk], k, v, gbd[chunk], allow)
        for h in range(GROUP):
            cut = slice(h * 2 * BLOCK, (h + 1) * 2 * BLOCK)
            ds = dscore[:, cut]
            pack_ref[base + h * BLOCK : base + (h + 1) * BLOCK, :] = jnp.where(
                row <= lane, probs_b[:, cut].astype(jnp.float32), turn(fold, ds)
            ).astype(jnp.bfloat16)
            diag.append(
                jnp.sum(jnp.where(row == lane, ds.astype(jnp.float32), 0.0), axis=0, keepdims=True)
            )
        for i, part in enumerate((k, v, dk, dv)):
            for j in range(2):
                r = base + AT + i * SIDE + j * BLOCK
                pack_ref[r : r + BLOCK, :] = part[:, j * HD : (j + 1) * HD]
    diag.append(jnp.zeros((DIAG - 2 * GROUP, 2 * BLOCK), jnp.float32))
    pack_ref[2 * ROWS :, :] = jnp.concatenate(diag, 0).astype(jnp.bfloat16)


def make_pack(bits, first, valid, plan, q, k, v, g):
    hbm = pl.BlockSpec(memory_space=pltpu.HBM)
    vmem = pl.BlockSpec(memory_space=pltpu.VMEM)
    return pl.pallas_call(
        functools.partial(pack_kernel, bits),
        out_shape=[
            pltpu.VMEM((2 * ROWS + DIAG, HD), jnp.bfloat16),
            pltpu.VMEM((3, 1, HD), jnp.int32),
            pltpu.VMEM((5, 1, HD), jnp.int32),
        ],
        in_specs=[hbm] * 7,
        out_specs=[vmem] * 3,
        scratch_shapes=[
            pltpu.SMEM(first.shape, jnp.int32),
            pltpu.SMEM(valid.shape, jnp.int32),
            pltpu.SMEM(plan.shape, jnp.int32),
            pltpu.VMEM((2, GROUP * 2 * BLOCK, 2 * HD), jnp.bfloat16),
            pltpu.VMEM((2, GROUP * 2 * BLOCK, 2 * HD), jnp.bfloat16),
            pltpu.SemaphoreType.DMA((3, 4)),
        ]
        + [pltpu.VMEM((BLOCK, x.shape[1]), x.dtype) for x in (q, k, v, g)],
        compiler_params=pltpu.CompilerParams(vmem_limit_bytes=VMEM_LIMIT),
        cost_estimate=pl.CostEstimate(
            flops=16 * BLOCK * GROUP * 2 * BLOCK * 2 * HD, bytes_accessed=3 << 20, transcendentals=0
        ),
        name="pack_rows",
    )(*(pltpu.with_memory_space_constraint(x, pltpu.HBM) for x in (first, valid, plan, q, k, v, g)))


def finish_kernel(facts_ref, pack, q_hbm, k_hbm, v_hbm, g_hbm, *refs):
    outs, ins, news = refs[:4], refs[4:8], refs[8:12]
    qbd, gbd, in_sem, out_sem = refs[12:]
    q_buf, k_buf, v_buf, g_buf = ins
    o_buf, dq_buf, dk_buf, dv_buf = news
    joined = jnp.max(facts_ref[1]) == 1

    def read(block):
        rows = pl.ds(block * BLOCK, BLOCK)
        return [
            pltpu.make_async_copy(hbm.at[rows, :], buf.at[rows, :], in_sem.at[block, i])
            for i, (hbm, buf) in enumerate(zip((q_hbm, k_hbm, v_hbm, g_hbm), ins))
        ]

    def write(block, part, parts):
        copies = []
        for i, (buf, out) in enumerate(zip(news, outs)):
            width = buf.shape[1] // parts
            at = (pl.ds(block * BLOCK, BLOCK), pl.ds(part * width, width))
            copies.append(
                pltpu.make_async_copy(buf.at[at], out.at[at], out_sem.at[2 * block + part, i])
            )
            copies[-1].start()
        return copies

    low, high = read(0), read(1)
    for c in low:
        c.start()

    @pl.when(joined)
    def _():
        for c in high:
            c.start()

    @pl.when(jnp.logical_not(joined))
    def _():
        fold = fold_matrix()
        square = (BLOCK, 2 * BLOCK)
        row, lane = iota(square, 0), iota(square, 1) & (BLOCK - 1)
        zero = jnp.zeros((BLOCK, HD), jnp.bfloat16)
        diag = pack[2 * ROWS :, :].astype(jnp.float32)
        copies = []
        for chunk in range(2):
            fill_zeros(qbd.at[chunk])
            fill_zeros(gbd.at[chunk])
        for chunk in range(2):
            base = chunk * ROWS

            def spread(i):
                r = base + AT + i * SIDE
                return jnp.concatenate(
                    [
                        jnp.concatenate([pack[r : r + BLOCK, :], zero], 1),
                        jnp.concatenate([zero, pack[r + BLOCK : r + SIDE, :]], 1),
                    ],
                    0,
                )

            kbd, vbd = spread(0), spread(1)
            for j in range(2):
                for i, buf in ((2, dk_buf), (3, dv_buf)):
                    r, at = base + AT + i * SIDE + j * BLOCK, (2 * chunk + j) * HD
                    buf[BLOCK:, at : at + HD] = pack[r : r + BLOCK, :]
            probs, dscore = [], []
            for h in range(GROUP):
                both = pack[base + h * BLOCK : base + (h + 1) * BLOCK, :].astype(jnp.float32)
                upper = jnp.where(row <= lane, both, 0.0).astype(jnp.bfloat16)
                probs.append(turn(fold, upper).astype(jnp.bfloat16))
                line = jnp.where(row == lane, diag[chunk * GROUP + h : chunk * GROUP + h + 1, :], 0.0)
                dscore.append(jnp.where(row > lane, both, line).astype(jnp.bfloat16))
            out = mm(jnp.concatenate(probs, 0), vbd, NN).astype(jnp.bfloat16)
            dq = mm(jnp.concatenate(dscore, 0), kbd, NN).astype(jnp.bfloat16)
            for buf, val in ((o_buf, out), (dq_buf, dq)):
                for h in range(GROUP):
                    for j in range(2):
                        at = chunk * PAIR + (j * GROUP + h) * HD
                        buf[BLOCK:, at : at + HD] = val[
                            h * BLOCK : (h + 1) * BLOCK, j * HD : (j + 1) * HD
                        ]
            copies += write(1, chunk, 2)
        for c in low:
            c.wait()
        allow = block_mask(jnp.max(facts_ref[2]))
        for chunk in range(2):
            heads = slice(chunk * PAIR, (chunk + 1) * PAIR)
            pair = slice(chunk * 2 * HD, (chunk + 1) * 2 * HD)
            fill_pair(qbd.at[chunk], q_buf.at[0:BLOCK, heads])
            fill_pair(gbd.at[chunk], g_buf.at[0:BLOCK, heads])
            k, v = k_buf[0:BLOCK, pair], v_buf[0:BLOCK, pair]
            probs_b, dscore, dk, dv = attend(qbd[chunk], k, v, gbd[chunk], allow)
            dk_buf[0:BLOCK, pair] = dk
            dv_buf[0:BLOCK, pair] = dv
            for buf, squares, other in ((o_buf, probs_b, v), (dq_buf, dscore, k)):
                turned = squares.T
                for j in range(2):
                    rows = [turned[(2 * h + j) * BLOCK : (2 * h + j + 1) * BLOCK] for h in range(GROUP)]
                    val = mm(jnp.concatenate(rows, 0), other[:, j * HD : (j + 1) * HD], NN).astype(jnp.bfloat16)
                    for h in range(GROUP):
                        at = chunk * PAIR + (j * GROUP + h) * HD
                        buf[0:BLOCK, at : at + HD] = val[h * BLOCK : (h + 1) * BLOCK]
            copies += write(0, chunk, 2)
        for c in copies:
            c.wait()

    @pl.when(joined)
    def _():
        for c in low + high:
            c.wait()
        wide = (SEQ, GROUP * SEQ)
        key_pos = iota(wide, 0)
        query_pos = iota(wide, 1) & (SEQ - 1)
        live_of = jnp.where(key_pos < BLOCK, jnp.max(facts_ref[2]), jnp.max(facts_ref[3]))
        allow = (key_pos <= query_pos) & ((key_pos & (BLOCK - 1)) < live_of)

        @pl.loop(0, KVH)
        def _(i):
            one = pl.ds(pl.multiple_of(i * HD, HD), HD)

            def head(h):
                return pl.ds(pl.multiple_of((i * GROUP + h) * HD, HD), HD)

            k, v = k_buf[:, one], v_buf[:, one]
            q = jnp.concatenate([q_buf[:, head(h)] for h in range(GROUP)], 0)
            g = jnp.concatenate([g_buf[:, head(h)] for h in range(GROUP)], 0)
            probs_b, dscore, dk, dv = attend(q, k, v, g, allow)
            dk_buf[:, one] = dk
            dv_buf[:, one] = dv
            for h in range(GROUP):
                cut = slice(h * SEQ, (h + 1) * SEQ)
                o_buf[:, head(h)] = mm(probs_b[:, cut], v, TN).astype(jnp.bfloat16)
                dq_buf[:, head(h)] = mm(dscore[:, cut], k, TN).astype(jnp.bfloat16)

        for c in write(0, 0, 1) + write(1, 0, 1):
            c.wait()


def finish(facts, pack, q, k, v, g):
    vmem = pl.BlockSpec(memory_space=pltpu.VMEM)
    hbm = pl.BlockSpec(memory_space=pltpu.HBM)
    return pl.pallas_call(
        finish_kernel,
        out_shape=[jax.ShapeDtypeStruct(x.shape, jnp.bfloat16) for x in (q, q, k, v)],
        in_specs=[vmem] * 2 + [hbm] * 4,
        out_specs=[hbm] * 4,
        scratch_shapes=[pltpu.VMEM(x.shape, jnp.bfloat16) for x in (q, k, v, g, q, q, k, v)]
        + [pltpu.VMEM((2, GROUP * 2 * BLOCK, 2 * HD), jnp.bfloat16)] * 2
        + [pltpu.SemaphoreType.DMA((2, 4)), pltpu.SemaphoreType.DMA((4, 4))],
        compiler_params=pltpu.CompilerParams(vmem_limit_bytes=VMEM_LIMIT),
        cost_estimate=pl.CostEstimate(
            flops=12 * KVH * GROUP * SEQ * SEQ * HD, bytes_accessed=4 << 20, transcendentals=0
        ),
        name="finish_rows",
    )(facts, pack, *(pltpu.with_memory_space_constraint(x, pltpu.HBM) for x in (q, k, v, g)))


def origins(branch):
    found = []
    for chip in range(4):
        crossed = branch >> (chip & 1) & 1
        passed = chip ^ 2 * crossed
        found.append(2 * crossed ^ (branch >> 2 + passed & 1))
    return found


def body(queries, keys, values, out_grad, doc_first, doc_valid, move_plan):
    core, dp = lax.axis_size("fsdp"), lax.axis_size("dp")
    near, far = 1, core * dp // 2
    bits = (near, core, far)
    args = (queries, keys, values, out_grad)
    first, valid, plan = doc_first.T, doc_valid.T, jnp.swapaxes(move_plan, 1, 2)
    pack, send, facts = make_pack(bits, first, valid, plan, *args)
    other = lax.ppermute(pack, "dp", [(i, i ^ 1) for i in range(dp)])

    def route(index):
        found = origins(index)

        def run(pack, other, send, facts):
            take = facts[0]
            got = []
            for step in (1, 3, 2) if found in ([3, 2, 3, 2], [2, 3, 2, 3]) else (1, 2, 3):
                if step not in found:
                    continue
                chips = [chip for chip in range(4) if found[chip] == step]
                if len(chips) == 3:
                    chips = [0, 1, 2, 3]
                pairs = []
                for i in range(core * dp):
                    if i // near % 2 + 2 * (i // far % 2) in chips:
                        pairs.append((i ^ (step & 1) * near ^ (step >> 1) * far, i))
                sent = jnp.where(send[step - 1] == 1, other, pack)
                got.append((step, lax.ppermute(sent, ("dp", "fsdp"), pairs)))
            result = jnp.where(take == 1, other, pack)
            for step, rows in got:
                result = jnp.where(take == step + 1, rows, result)
            return result

        return run

    rows = lax.switch(facts[4, 0, 0], [route(i) for i in range(64)], pack, other, send, facts)
    return tuple(finish(facts, rows, *args))


def solution(mesh):
    rows = P(("dp", "fsdp"), None)
    return jax.shard_map(
        body,
        mesh=mesh,
        in_specs=(rows,) * 4 + (P(),) * 3,
        out_specs=(rows,) * 4,
        check_vma=False,
    )
```

```python
import functools

import jax
import jax.numpy as jnp
from jax import lax
from jax.experimental import pallas as pl
from jax.experimental.pallas import tpu as pltpu
from jax.sharding import PartitionSpec as P

HD = 128
KVH = 4
GROUP = 7
BLOCK = 64
SEQ = 2 * BLOCK
SCALE = 1.0 / HD**0.5
PAIR = 2 * GROUP * HD
TRI = GROUP * BLOCK
DIAG = 16
SIDE = 2 * BLOCK
ROWS = TRI + 4 * SIDE
AT = TRI
VMEM_LIMIT = 40 * 1024 * 1024

NT = (((1,), (1,)), ((), ()))
NN = (((1,), (0,)), ((), ()))
TN = (((0,), (0,)), ((), ()))


def mm(a, b, dims):
    return lax.dot_general(a, b, dims, preferred_element_type=jnp.float32)


def iota(shape, dim):
    return lax.broadcasted_iota(jnp.int32, shape, dim)


def fold_matrix():
    shape = (BLOCK, 2 * BLOCK)
    return jnp.where((iota(shape, 1) & (BLOCK - 1)) == iota(shape, 0), 1.0, 0.0).astype(jnp.bfloat16)


def turn(fold, pair):
    low = iota(pair.shape, 1) < BLOCK
    zero = jnp.zeros_like(pair)
    split = jnp.concatenate([jnp.where(low, pair, zero), jnp.where(low, zero, pair)], 0)
    return mm(fold, split, NT)


def read_moves(plan_ref, near, core, far):
    me = lax.axis_index("dp") * core + lax.axis_index("fsdp")
    base = me & ~(near + far)
    z, c = [], []
    for q in range(4):
        at = base + (q & 1) * near + (q >> 1) * far
        c.append(plan_ref[1, 1, at])
        z.append(plan_ref[0, 1, at ^ (c[q] * core)])
    y = [plan_ref[2, 1, base], plan_ref[2, 1, base + near]]
    here = ((me // near) & 1) + 2 * ((me // far) & 1)

    def pick(values, index):
        out = values[0]
        for i in range(1, len(values)):
            out = jnp.where(index == i, values[i], out)
        return out

    def origin(chip):
        crossed = pick(y, chip & 1)
        passed = chip ^ (2 * crossed)
        return pick(z, passed) ^ (2 * crossed), pick(c, passed)

    branch = y[0] + 2 * y[1] + 4 * z[0] + 8 * z[1] + 16 * z[2] + 32 * z[3]
    send = [origin(here ^ step)[1] for step in range(1, 4)]
    mine, other = origin(here)
    take = jnp.where(mine == 0, other, mine + 1)

    return branch, send, take


def fill_zeros(full):
    zero = jnp.zeros((BLOCK, HD), jnp.bfloat16)
    for h in range(GROUP):
        r = h * 2 * BLOCK
        full[r : r + BLOCK, HD:] = zero
        full[r + BLOCK : r + 2 * BLOCK, 0:HD] = zero


def fill_pair(full, rows):
    for h in range(GROUP):
        r = h * 2 * BLOCK
        full[r : r + BLOCK, 0:HD] = rows[:, h * HD : (h + 1) * HD]
        full[r + BLOCK : r + 2 * BLOCK, HD:] = rows[:, (GROUP + h) * HD : (GROUP + h + 1) * HD]


def attend(q, k, v, g, allow):
    score = jnp.where(allow, mm(k, q, NT) * SCALE, -1e30)
    weights = jnp.exp(score - jnp.max(score, axis=0, keepdims=True))
    probs = weights * (1.0 / jnp.sum(weights, axis=0, keepdims=True))
    probs_b = probs.astype(jnp.bfloat16)
    dprob = mm(v, g, NT)
    delta = jnp.sum(probs * dprob, axis=0, keepdims=True)
    dscore = (probs * (dprob - delta) * SCALE).astype(jnp.bfloat16)
    dv = mm(probs_b, g, NN).astype(jnp.bfloat16)
    dk = mm(dscore, q, NN).astype(jnp.bfloat16)
    return probs_b, dscore, dk, dv


def block_mask(live):
    wide = (BLOCK, GROUP * 2 * BLOCK)
    key_pos = iota(wide, 0)
    query_pos = iota(wide, 1) & (BLOCK - 1)
    return (key_pos <= query_pos) & (key_pos < live)


def pack_kernel(bits, first_hbm, valid_hbm, plan_hbm, q_hbm, k_hbm, v_hbm, g_hbm, *refs):
    pack_ref, send_ref, facts_ref = refs[:3]
    first_ref, valid_ref, plan_ref, qbd, gbd, sem = refs[3:9]
    bufs = refs[9:]
    q_buf, k_buf, v_buf, g_buf = bufs
    words = [
        pltpu.make_async_copy(hbm, ref, sem.at[2, i])
        for i, (hbm, ref) in enumerate(
            ((plan_hbm, plan_ref), (valid_hbm, valid_ref), (first_hbm, first_ref))
        )
    ]
    copies = []
    for chunk in range(2):
        for i, (hbm, buf) in enumerate(zip((q_hbm, k_hbm, v_hbm, g_hbm), bufs)):
            width = buf.shape[1] // 2
            cut = pl.ds(chunk * width, width)
            copies.append(
                pltpu.make_async_copy(
                    hbm.at[pl.ds(BLOCK, BLOCK), cut], buf.at[:, cut], sem.at[chunk, i]
                )
            )
    for c in words + copies:
        c.start()
    for chunk in range(2):
        fill_zeros(qbd.at[chunk])
        fill_zeros(gbd.at[chunk])
    for c in words:
        c.wait()
    branch, send, take = read_moves(plan_ref, *bits)
    me = lax.axis_index("dp") * bits[1] + lax.axis_index("fsdp")
    for i in range(3):
        send_ref[i] = jnp.full((1, HD), send[i], jnp.int32)
    facts = (take, jnp.where(first_ref[1, me] == 0, 1, 0), valid_ref[0, me], valid_ref[1, me], branch)
    for i, fact in enumerate(facts):
        facts_ref[i] = jnp.full((1, HD), fact, jnp.int32)
    allow = block_mask(valid_ref[1, me])
    fold = fold_matrix()
    square = (BLOCK, 2 * BLOCK)
    row, lane = iota(square, 0), iota(square, 1) & (BLOCK - 1)
    diag = []
    for chunk in range(2):
        for c in copies[4 * chunk : 4 * chunk + 4]:
            c.wait()
        base = chunk * ROWS
        heads = slice(chunk * PAIR, (chunk + 1) * PAIR)
        pair = slice(chunk * 2 * HD, (chunk + 1) * 2 * HD)
        fill_pair(qbd.at[chunk], q_buf.at[:, heads])
        fill_pair(gbd.at[chunk], g_buf.at[:, heads])
        k, v = k_buf[:, pair], v_buf[:, pair]
        probs_b, dscore, dk, dv = attend(qbd[chunk], k, v, gbd[chunk], allow)
        for h in range(GROUP):
            cut = slice(h * 2 * BLOCK, (h + 1) * 2 * BLOCK)
            ds = dscore[:, cut]
            pack_ref[base + h * BLOCK : base + (h + 1) * BLOCK, :] = jnp.where(
                row <= lane, probs_b[:, cut].astype(jnp.float32), turn(fold, ds)
            ).astype(jnp.bfloat16)
            diag.append(
                jnp.sum(jnp.where(row == lane, ds.astype(jnp.float32), 0.0), axis=0, keepdims=True)
            )
        for i, part in enumerate((k, v, dk, dv)):
            for j in range(2):
                r = base + AT + i * SIDE + j * BLOCK
                pack_ref[r : r + BLOCK, :] = part[:, j * HD : (j + 1) * HD]
    diag.append(jnp.zeros((DIAG - 2 * GROUP, 2 * BLOCK), jnp.float32))
    pack_ref[2 * ROWS :, :] = jnp.concatenate(diag, 0).astype(jnp.bfloat16)


def make_pack(bits, first, valid, plan, q, k, v, g):
    hbm = pl.BlockSpec(memory_space=pltpu.HBM)
    vmem = pl.BlockSpec(memory_space=pltpu.VMEM)
    return pl.pallas_call(
        functools.partial(pack_kernel, bits),
        out_shape=[
            pltpu.VMEM((2 * ROWS + DIAG, HD), jnp.bfloat16),
            pltpu.VMEM((3, 1, HD), jnp.int32),
            pltpu.VMEM((5, 1, HD), jnp.int32),
        ],
        in_specs=[hbm] * 7,
        out_specs=[vmem] * 3,
        scratch_shapes=[
            pltpu.SMEM(first.shape, jnp.int32),
            pltpu.SMEM(valid.shape, jnp.int32),
            pltpu.SMEM(plan.shape, jnp.int32),
            pltpu.VMEM((2, GROUP * 2 * BLOCK, 2 * HD), jnp.bfloat16),
            pltpu.VMEM((2, GROUP * 2 * BLOCK, 2 * HD), jnp.bfloat16),
            pltpu.SemaphoreType.DMA((3, 4)),
        ]
        + [pltpu.VMEM((BLOCK, x.shape[1]), x.dtype) for x in (q, k, v, g)],
        compiler_params=pltpu.CompilerParams(vmem_limit_bytes=VMEM_LIMIT),
        cost_estimate=pl.CostEstimate(
            flops=16 * BLOCK * GROUP * 2 * BLOCK * 2 * HD, bytes_accessed=3 << 20, transcendentals=0
        ),
        name="pack_rows",
    )(*(pltpu.with_memory_space_constraint(x, pltpu.HBM) for x in (first, valid, plan, q, k, v, g)))


def finish_kernel(facts_ref, pack, q_hbm, k_hbm, v_hbm, g_hbm, *refs):
    outs, ins, news = refs[:4], refs[4:8], refs[8:12]
    qbd, gbd, in_sem, out_sem = refs[12:]
    q_buf, k_buf, v_buf, g_buf = ins
    o_buf, dq_buf, dk_buf, dv_buf = news
    joined = jnp.max(facts_ref[1]) == 1

    def read(block):
        rows = pl.ds(block * BLOCK, BLOCK)
        return [
            pltpu.make_async_copy(hbm.at[rows, :], buf.at[rows, :], in_sem.at[block, i])
            for i, (hbm, buf) in enumerate(zip((q_hbm, k_hbm, v_hbm, g_hbm), ins))
        ]

    def write(block, part, parts):
        copies = []
        for i, (buf, out) in enumerate(zip(news, outs)):
            width = buf.shape[1] // parts
            at = (pl.ds(block * BLOCK, BLOCK), pl.ds(part * width, width))
            copies.append(
                pltpu.make_async_copy(buf.at[at], out.at[at], out_sem.at[2 * block + part, i])
            )
            copies[-1].start()
        return copies

    low, high = read(0), read(1)
    for c in low:
        c.start()

    @pl.when(joined)
    def _():
        for c in high:
            c.start()

    @pl.when(jnp.logical_not(joined))
    def _():
        square = (BLOCK, 2 * BLOCK)
        row, lane = iota(square, 0), iota(square, 1) & (BLOCK - 1)
        zero = jnp.zeros((BLOCK, HD), jnp.bfloat16)
        diag = pack[2 * ROWS :, :].astype(jnp.float32)
        copies = []
        for chunk in range(2):
            fill_zeros(qbd.at[chunk])
            fill_zeros(gbd.at[chunk])
        for chunk in range(2):
            base = chunk * ROWS

            def spread(i):
                r = base + AT + i * SIDE
                return jnp.concatenate(
                    [
                        jnp.concatenate([pack[r : r + BLOCK, :], zero], 1),
                        jnp.concatenate([zero, pack[r + BLOCK : r + SIDE, :]], 1),
                    ],
                    0,
                )

            kbd = spread(0)
            for j in range(2):
                for i, buf in ((2, dk_buf), (3, dv_buf)):
                    r, at = base + AT + i * SIDE + j * BLOCK, (2 * chunk + j) * HD
                    buf[BLOCK:, at : at + HD] = pack[r : r + BLOCK, :]
            probs, dscore = [], []
            for h in range(GROUP):
                both = pack[base + h * BLOCK : base + (h + 1) * BLOCK, :].astype(jnp.float32)
                upper = jnp.where(row <= lane, both, 0.0).astype(jnp.bfloat16)
                probs.append(upper.T)
                line = jnp.where(row == lane, diag[chunk * GROUP + h : chunk * GROUP + h + 1, :], 0.0)
                dscore.append(jnp.where(row > lane, both, line).astype(jnp.bfloat16))
            out = []
            for j in range(2):
                part = jnp.concatenate([p[j * BLOCK : (j + 1) * BLOCK] for p in probs], 0)
                r = base + AT + SIDE + j * BLOCK
                out.append(mm(part, pack[r : r + BLOCK, :], NN).astype(jnp.bfloat16))
            out = jnp.concatenate(out, 1)
            dq = mm(jnp.concatenate(dscore, 0), kbd, NN).astype(jnp.bfloat16)
            for buf, val in ((o_buf, out), (dq_buf, dq)):
                for h in range(GROUP):
                    for j in range(2):
                        at = chunk * PAIR + (j * GROUP + h) * HD
                        buf[BLOCK:, at : at + HD] = val[
                            h * BLOCK : (h + 1) * BLOCK, j * HD : (j + 1) * HD
                        ]
            copies += write(1, chunk, 2)
        for c in low:
            c.wait()
        allow = block_mask(jnp.max(facts_ref[2]))
        for chunk in range(2):
            heads = slice(chunk * PAIR, (chunk + 1) * PAIR)
            pair = slice(chunk * 2 * HD, (chunk + 1) * 2 * HD)
            fill_pair(qbd.at[chunk], q_buf.at[0:BLOCK, heads])
            fill_pair(gbd.at[chunk], g_buf.at[0:BLOCK, heads])
            k, v = k_buf[0:BLOCK, pair], v_buf[0:BLOCK, pair]
            probs_b, dscore, dk, dv = attend(qbd[chunk], k, v, gbd[chunk], allow)
            dk_buf[0:BLOCK, pair] = dk
            dv_buf[0:BLOCK, pair] = dv
            for buf, squares, other in ((o_buf, probs_b, v), (dq_buf, dscore, k)):
                turned = squares.T
                for j in range(2):
                    rows = [turned[(2 * h + j) * BLOCK : (2 * h + j + 1) * BLOCK] for h in range(GROUP)]
                    val = mm(jnp.concatenate(rows, 0), other[:, j * HD : (j + 1) * HD], NN).astype(jnp.bfloat16)
                    for h in range(GROUP):
                        at = chunk * PAIR + (j * GROUP + h) * HD
                        buf[0:BLOCK, at : at + HD] = val[h * BLOCK : (h + 1) * BLOCK]
            copies += write(0, chunk, 2)
        for c in copies:
            c.wait()

    @pl.when(joined)
    def _():
        for c in low + high:
            c.wait()
        wide = (SEQ, GROUP * SEQ)
        key_pos = iota(wide, 0)
        query_pos = iota(wide, 1) & (SEQ - 1)
        live_of = jnp.where(key_pos < BLOCK, jnp.max(facts_ref[2]), jnp.max(facts_ref[3]))
        allow = (key_pos <= query_pos) & ((key_pos & (BLOCK - 1)) < live_of)

        @pl.loop(0, KVH)
        def _(i):
            one = pl.ds(pl.multiple_of(i * HD, HD), HD)

            def head(h):
                return pl.ds(pl.multiple_of((i * GROUP + h) * HD, HD), HD)

            k, v = k_buf[:, one], v_buf[:, one]
            q = jnp.concatenate([q_buf[:, head(h)] for h in range(GROUP)], 0)
            g = jnp.concatenate([g_buf[:, head(h)] for h in range(GROUP)], 0)
            probs_b, dscore, dk, dv = attend(q, k, v, g, allow)
            dk_buf[:, one] = dk
            dv_buf[:, one] = dv
            for h in range(GROUP):
                cut = slice(h * SEQ, (h + 1) * SEQ)
                o_buf[:, head(h)] = mm(probs_b[:, cut], v, TN).astype(jnp.bfloat16)
                dq_buf[:, head(h)] = mm(dscore[:, cut], k, TN).astype(jnp.bfloat16)

        for c in write(0, 0, 1) + write(1, 0, 1):
            c.wait()


def finish(facts, pack, q, k, v, g):
    vmem = pl.BlockSpec(memory_space=pltpu.VMEM)
    hbm = pl.BlockSpec(memory_space=pltpu.HBM)
    return pl.pallas_call(
        finish_kernel,
        out_shape=[jax.ShapeDtypeStruct(x.shape, jnp.bfloat16) for x in (q, q, k, v)],
        in_specs=[vmem] * 2 + [hbm] * 4,
        out_specs=[hbm] * 4,
        scratch_shapes=[pltpu.VMEM(x.shape, jnp.bfloat16) for x in (q, k, v, g, q, q, k, v)]
        + [pltpu.VMEM((2, GROUP * 2 * BLOCK, 2 * HD), jnp.bfloat16)] * 2
        + [pltpu.SemaphoreType.DMA((2, 4)), pltpu.SemaphoreType.DMA((4, 4))],
        compiler_params=pltpu.CompilerParams(vmem_limit_bytes=VMEM_LIMIT),
        cost_estimate=pl.CostEstimate(
            flops=12 * KVH * GROUP * SEQ * SEQ * HD, bytes_accessed=4 << 20, transcendentals=0
        ),
        name="finish_rows",
    )(facts, pack, *(pltpu.with_memory_space_constraint(x, pltpu.HBM) for x in (q, k, v, g)))


def origins(branch):
    found = []
    for chip in range(4):
        crossed = branch >> (chip & 1) & 1
        passed = chip ^ 2 * crossed
        found.append(2 * crossed ^ (branch >> 2 + passed & 1))
    return found


def body(queries, keys, values, out_grad, doc_first, doc_valid, move_plan):
    core, dp = lax.axis_size("fsdp"), lax.axis_size("dp")
    near, far = 1, core * dp // 2
    bits = (near, core, far)
    args = (queries, keys, values, out_grad)
    first, valid, plan = doc_first.T, doc_valid.T, jnp.swapaxes(move_plan, 1, 2)
    pack, send, facts = make_pack(bits, first, valid, plan, *args)
    other = lax.ppermute(pack, "dp", [(i, i ^ 1) for i in range(dp)])

    def route(index):
        found = origins(index)

        def run(pack, other, send, facts):
            take = facts[0]
            got = []
            for step in (1, 3, 2) if found in ([3, 2, 3, 2], [2, 3, 2, 3]) else (1, 2, 3):
                if step not in found:
                    continue
                chips = [chip for chip in range(4) if found[chip] == step]
                if len(chips) == 3:
                    chips = [0, 1, 2, 3]
                pairs = []
                for i in range(core * dp):
                    if i // near % 2 + 2 * (i // far % 2) in chips:
                        pairs.append((i ^ (step & 1) * near ^ (step >> 1) * far, i))
                sent = jnp.where(send[step - 1] == 1, other, pack)
                got.append((step, lax.ppermute(sent, ("dp", "fsdp"), pairs)))
            result = jnp.where(take == 1, other, pack)
            for step, rows in got:
                result = jnp.where(take == step + 1, rows, result)
            return result

        return run

    rows = lax.switch(facts[4, 0, 0], [route(i) for i in range(64)], pack, other, send, facts)
    return tuple(finish(facts, rows, *args))


def solution(mesh):
    rows = P(("dp", "fsdp"), None)
    return jax.shard_map(
        body,
        mesh=mesh,
        in_specs=(rows,) * 4 + (P(),) * 3,
        out_specs=(rows,) * 4,
        check_vma=False,
    )
```
